128 devices in a mesh: grp: 4 (over x), seq: 32 (over z, y, core).
Axes of the slice: x: 4, y: 4, z: 4, core: 2. Of those that a mesh axis runs over, the one named last changes fastest.
Arguments:
- captions: bfloat16 [2048, 4096], P(('grp', 'seq')), may hold values from -6 to 6
- lengths: int32 [4, 8], replicated, may hold values from 1 to 300, 512 in all within a row
- clip_order: int32 [32], replicated, may hold values from 0 to 31, each once
- t5_gain: float32 [4096], replicated, may hold values from 0.5 to 1.5
- w_tq: bfloat16 [4096, 4096], P(None, 'seq'), may hold values from -0.13671875 to 0.13671875
- w_tk: bfloat16 [4096, 4096], P(None, 'seq'), may hold values from -0.09375 to 0.09375
- w_tv: bfloat16 [4096, 4096], P(None, 'seq'), may hold values from -0.09375 to 0.09375
- w_to: bfloat16 [4096, 4096], P('seq'), may hold values from -0.09375 to 0.09375
- w_kv: bfloat16 [4096, 2304], P(None, 'seq'), may hold values from -0.09375 to 0.09375
- video: bfloat16 [32, 2048, 1152], P('grp', 'seq'), may hold values from -6 to 6
- modulation: float32 [32, 3, 1152], P('grp'), may hold values from -4 to 4
- w_qkv: bfloat16 [1152, 3456], replicated, may hold values from -1.5320647 to 1.5320647
- w_o: bfloat16 [1152, 1152], replicated, may hold values from -0.1875 to 0.1875
- w_cq: bfloat16 [1152, 1152], replicated, may hold values from -2.0623948 to 2.0623948
- w_co: bfloat16 [1152, 1152], replicated, may hold values from -0.1875 to 0.1875
Outputs:
- video_out: bfloat16 [32, 2048, 1152], P('grp', 'seq')
The draws below stay inside these ranges and needn't reach their ends.
Inputs may be any that keep to these rules, and one draw needn't show every extreme that they name: `lengths`: each row sums to 512, and the largest entry of each row is 300. `clip_order`: every clip is described by exactly one caption.
All inputs are finite; a program needn't handle non-finite values.
Results may differ from the reference program's by a relative error of at most 0.029.
The reference program's roundings to bfloat16 on the way count: a program that leaves them out, or rounds other values in their place, can miss the bound.
Values may be sent and summed in bfloat16 or wider, within the bound.
A program may use at most 320 MiB of HBM per device.

```python
import math
import jax
import jax.numpy as jnp
import numpy as np
from jax import lax

DT = 4096
HT = 64
ET = 64
D = 1152
H = 16
E = 72
CLIP_GRP = 8
PACK = 512
LMAX = 300
VT = 2048
N_CLIPS = 32
N_GRP = 4


def draw_w_tq(key, part):
    key = jax.random.fold_in(key, 11)
    base = (DT * ET) ** (-0.5)
    values = jnp.clip(jax.random.normal(key, (DT, DT), jnp.float32), -6.0, 6.0) * (2.0 * base)
    return values.astype(jnp.bfloat16)


def draw_w_qkv(key, part):
    key = jax.random.fold_in(key, 23)
    base = D ** (-0.5)
    column = jnp.arange(3 * D)
    factor = jnp.where(column < D, 3.0, 1.0) * base
    values = jnp.clip(jax.random.normal(key, (D, 3 * D), jnp.float32), -6.0, 6.0) * factor[None, :]
    return values.astype(jnp.bfloat16)


def draw_w_cq(key, part):
    key = jax.random.fold_in(key, 37)
    base = D ** (-0.5)
    values = jnp.clip(jax.random.normal(key, (D, D), jnp.float32), -6.0, 6.0) * (2.0 * base)
    return values.astype(jnp.bfloat16)


def block_levels(key, dims, split, least, top_value):
    def one(dim, parts):
        heights = jax.random.uniform(jax.random.fold_in(jax.random.fold_in(key, 6), dim), (parts,), jnp.float32, least / len(split), top_value / len(split))
        return jnp.repeat(jnp.exp(heights), dims[dim] // parts).reshape((-1,) + (1,) * (len(dims) - dim - 1))

    level = one(*split[0])
    for cut in split[1:]:
        level = level * one(*cut)
    return level


def profile(number_of, total, limit, lean):
    portions = [(1 << 20) // math.isqrt(rank ** lean) + 1 for rank in range(2, number_of + 1)]
    surplus, holding = total - limit - (number_of - 1), [1] * (number_of - 1)
    while surplus > 0:
        movable = [i for i in range(number_of - 1) if holding[i] < limit]
        pool, left = sum([portions[i] for i in movable]), surplus
        for i in movable:
            addition = min(limit - holding[i], max(1, left * portions[i] // pool), surplus)
            holding[i] = holding[i] + addition
            surplus = surplus - addition
    return np.array([limit] + holding)


def uneven_parts(stream_key, count, total, reach, slope):
    if count == 2:
        one = jax.random.randint(stream_key, (), max(1, total - reach), min(reach, total - 1) + 1)
        return jnp.stack([one, total - one])
    tallies = jnp.asarray(profile(count, total, reach, slope), jnp.int32)
    pairs = (count - 1) // 2
    source_of, receiver = tallies[1:1 + 2 * pairs:2], tallies[2:2 + 2 * pairs:2]
    margin = jnp.minimum(source_of - 1, reach - receiver)
    shifted = jax.random.randint(jax.random.fold_in(stream_key, 1), (pairs,), 0, 1 << 20) % (margin + 1)
    tallies = tallies.at[1:1 + 2 * pairs:2].set(source_of - shifted).at[2:2 + 2 * pairs:2].set(receiver + shifted)
    return tallies[jax.random.permutation(jax.random.fold_in(stream_key, 2), count)]


def noise(own_key, extent, scale, reach, split=(), kind=jnp.bfloat16):
    drawn = scale * jax.random.normal(own_key, extent, jnp.float32)
    if split:
        drawn = drawn * block_levels(own_key, extent, split, -0.22, 0.18)
    return jnp.clip(drawn, -reach, reach).astype(kind)


def setup_inputs(seed: int = 0) -> dict:
    key_of = jax.random.split(jax.random.key(seed), 16)
    captions = noise(key_of[0], (N_GRP * PACK, DT), 1.0, 6.0, ((0, 128),))
    lengths = jax.vmap(lambda own: uneven_parts(own, CLIP_GRP, PACK, LMAX, 2))(jax.random.split(key_of[1], N_GRP)).reshape((N_GRP, CLIP_GRP)).astype(jnp.int32)
    clip_order = jax.random.permutation(key_of[2], N_CLIPS).astype(jnp.int32)
    t5_gain = jnp.clip(1.0 + 0.1 * jax.random.normal(key_of[3], (DT,), jnp.float32), 0.5, 1.5)
    w_tq = draw_w_tq(jax.random.fold_in(key_of[15], 71), 0)
    w_tk = noise(key_of[5], (DT, DT), DT ** -0.5, 0.09375, ((1, 32),))
    w_tv = noise(key_of[6], (DT, DT), DT ** -0.5, 0.09375, ((1, 32),))
    w_to = noise(key_of[7], (DT, DT), DT ** -0.5, 0.09375, ((0, 32),))
    w_kv = noise(key_of[8], (DT, 2 * D), DT ** -0.5, 0.09375, ((1, 32),))
    video = noise(key_of[9], (N_CLIPS, VT, D), 1.0, 6.0, ((0, 4), (1, 32)))
    modulation = noise(key_of[10], (N_CLIPS, 3, D), 1.0, 4.0, ((0, 4),), jnp.float32)
    w_qkv = draw_w_qkv(jax.random.fold_in(key_of[15], 71), 0)
    w_o = noise(key_of[12], (D, D), D ** -0.5, 0.1875)
    w_cq = draw_w_cq(jax.random.fold_in(key_of[15], 71), 0)
    w_co = noise(key_of[14], (D, D), D ** -0.5, 0.1875)
    return {"captions": captions, "lengths": lengths, "clip_order": clip_order, "t5_gain": t5_gain, "w_tq": w_tq, "w_tk": w_tk, "w_tv": w_tv, "w_to": w_to, "w_kv": w_kv, "video": video, "modulation": modulation, "w_qkv": w_qkv, "w_o": w_o, "w_cq": w_cq, "w_co": w_co}


def widen(values):
    return lax.optimization_barrier(values).astype(jnp.float32)

def rms_rows(rows, gain):
    values = rows.astype(jnp.float32)
    power = lax.optimization_barrier(jnp.mean(values * values, axis=-1, keepdims=True))
    return (values * lax.rsqrt(power + 1e-06) * gain).astype(jnp.bfloat16)

def modulated_norm(rows, shift, scale):
    values = rows.astype(jnp.float32)
    center = values - lax.optimization_barrier(jnp.mean(values, axis=-1, keepdims=True))
    spread = lax.optimization_barrier(jnp.mean(center * center, axis=-1, keepdims=True))
    return (center * lax.rsqrt(spread + 1e-06) * (1.0 + scale) + shift).astype(jnp.bfloat16)

def masked_weights(score, keep):
    masked = jnp.where(keep, score, -1e+30)
    highest = lax.optimization_barrier(jnp.max(masked, axis=-1, keepdims=True))
    weight = jnp.where(keep, jnp.exp(masked - highest), 0.0)
    return (weight, lax.optimization_barrier(jnp.sum(weight, axis=-1, keepdims=True)))

def encode_pack(rows, pack_lengths, t5_gain, w_tq, w_tk, w_tv, w_to, w_kv):
    normed = rms_rows(rows, t5_gain)
    query = jnp.dot(normed, w_tq, preferred_element_type=jnp.float32).astype(jnp.bfloat16).reshape(PACK, HT, ET)
    key_rows = jnp.dot(normed, w_tk, preferred_element_type=jnp.float32).astype(jnp.bfloat16).reshape(PACK, HT, ET)
    value_rows = jnp.dot(normed, w_tv, preferred_element_type=jnp.float32).astype(jnp.bfloat16).reshape(PACK, HT, ET)
    ends = jnp.cumsum(pack_lengths).astype(jnp.int32)
    position = jnp.arange(PACK, dtype=jnp.int32)
    segment = lax.optimization_barrier(jnp.sum((position[:, None] >= ends[None, :]).astype(jnp.int32), axis=1))
    same = (segment[:, None] == segment[None, :])[None]
    score = jnp.einsum('qhe,khe->hqk', widen(query), widen(key_rows))
    weight, total = masked_weights(score, same)
    mixed = jnp.einsum('hqk,khe->hqe', widen(weight.astype(jnp.bfloat16)), widen(value_rows)) / total
    mixed = mixed.astype(jnp.bfloat16)
    flat = jnp.transpose(mixed, (1, 0, 2)).reshape(PACK, DT)
    encoded = (rows.astype(jnp.float32) + jnp.dot(flat, w_to, preferred_element_type=jnp.float32)).astype(jnp.bfloat16)
    return jnp.dot(encoded, w_kv, preferred_element_type=jnp.float32).astype(jnp.bfloat16)

def self_head(operands):
    query, key_rows, value_rows = operands
    score = jnp.dot(query, key_rows.T, preferred_element_type=jnp.float32) * E ** (-0.5)
    highest = lax.optimization_barrier(jnp.max(score, axis=-1, keepdims=True))
    weight = jnp.exp(score - highest)
    total = lax.optimization_barrier(jnp.sum(weight, axis=-1, keepdims=True))
    mixed = jnp.dot(weight.astype(jnp.bfloat16), value_rows, preferred_element_type=jnp.float32) / total
    return mixed.astype(jnp.bfloat16)

def reference(captions, lengths, clip_order, t5_gain, w_tq, w_tk, w_tv, w_to, w_kv, video, modulation, w_qkv, w_o, w_cq, w_co):
    packs = captions.reshape(N_GRP, PACK, DT)
    context = jnp.stack([encode_pack(packs[index], lengths[index], t5_gain, w_tq, w_tk, w_tv, w_to, w_kv) for index in range(N_GRP)])
    clip_count = clip_order.shape[0]
    clip_ids = jnp.arange(clip_count, dtype=jnp.int32)
    match = clip_order[None, :] == clip_ids[:, None]
    caption = lax.optimization_barrier(jnp.sum(jnp.where(match, clip_ids[None, :], 0), axis=1)).astype(jnp.int32)
    flat_length = lengths.reshape(-1)
    flat_end = jnp.cumsum(lengths, axis=1).astype(jnp.int32).reshape(-1)
    cap_length = flat_length[caption]
    cap_start = flat_end[caption] - cap_length
    source = (caption // CLIP_GRP).astype(jnp.int32)
    position = jnp.minimum(cap_start[:, None] + jnp.arange(LMAX, dtype=jnp.int32)[None, :], PACK - 1).astype(jnp.int32)
    picked = context[source[:, None], position]

    def one_clip(operands):
        frames, mods, chosen, length = operands
        normed = modulated_norm(frames, mods[0], mods[1])
        projected = jnp.dot(normed, w_qkv, preferred_element_type=jnp.float32).astype(jnp.bfloat16).reshape(VT, 3, H, E)
        heads = jnp.transpose(projected, (1, 2, 0, 3))
        mixed = lax.map(self_head, (heads[0], heads[1], heads[2]))
        flat = jnp.transpose(mixed, (1, 0, 2)).reshape(VT, D)
        attended = jnp.dot(flat, w_o, preferred_element_type=jnp.float32)
        hidden = (frames.astype(jnp.float32) + mods[2] * attended).astype(jnp.bfloat16)
        cross_query = jnp.dot(hidden, w_cq, preferred_element_type=jnp.float32).astype(jnp.bfloat16).reshape(VT, H, E)
        cross_key = chosen[:, :D].reshape(LMAX, H, E)
        cross_value = chosen[:, D:].reshape(LMAX, H, E)
        score = jnp.einsum('the,phe->htp', widen(cross_query), widen(cross_key)) * E ** (-0.5)
        keep = (jnp.arange(LMAX, dtype=jnp.int32) < length)[None, None, :]
        weight, total = masked_weights(score, keep)
        cross_mix = jnp.einsum('htp,phe->hte', widen(weight.astype(jnp.bfloat16)), widen(cross_value)) / total
        cross_mix = cross_mix.astype(jnp.bfloat16)
        cross_flat = jnp.transpose(cross_mix, (1, 0, 2)).reshape(VT, D)
        result = hidden.astype(jnp.float32) + jnp.dot(cross_flat, w_co, preferred_element_type=jnp.float32)
        return result.astype(jnp.bfloat16)
    return lax.map(one_clip, (video, modulation, picked, cap_length))
```

```python
import functools
import math

import jax
import jax.numpy as jnp
from jax import lax
from jax.experimental import pallas as pl
from jax.experimental.pallas import tpu as pltpu
from jax.sharding import PartitionSpec as P

ET = 64
D = 1152
H = 16
E = 72
DT = 4096
HALF = DT // 2
LANE = 128
WIN = 384
HP = 4 * LANE
KEYS = 512
EP = 80
VT = 2048
MIB = 1024 * 1024
LOG2E = math.log2(math.e)
QSCALE = E ** (-0.5) * LOG2E
BF = jnp.bfloat16
F32 = jnp.float32
MESH = pl.DeviceIdType.MESH


def place():
    seq = lax.axis_index("seq")
    core = seq % 2
    chip = seq // 2
    return seq, core, chip, chip % 4, chip // 4


def remote(src, dst, send, recv, peer, axis="seq"):
    return pltpu.make_async_remote_copy(
        src_ref=src,
        dst_ref=dst,
        send_sem=send,
        recv_sem=recv,
        device_id={axis: peer},
        device_id_type=MESH,
    )


def greet(peer, axis="seq"):
    pl.semaphore_signal(
        pltpu.get_barrier_semaphore(), inc=1, device_id={axis: peer}, device_id_type=MESH
    )


def head_select(offset):
    row = lax.broadcasted_iota(jnp.int32, (WIN, HP), 0)
    col = lax.broadcasted_iota(jnp.int32, (WIN, HP), 1)
    head = col >> 7
    lane = col & 127
    hit = (row == offset + head * E + lane) & (lane < E)
    return jnp.where(hit, 1.0, 0.0).astype(BF)


def head_merge(offset):
    row = lax.broadcasted_iota(jnp.int32, (HP, WIN), 0)
    col = lax.broadcasted_iota(jnp.int32, (HP, WIN), 1)
    head = row >> 7
    lane = row & 127
    hit = (col == offset + head * E + lane) & (lane < E)
    return jnp.where(hit, 1.0, 0.0).astype(BF)


class Gather:
    def __init__(self, buf, send, recv):
        seq, core, chip, y, z = place()
        sib = seq + 1 - 2 * core
        first = buf.at[z, y, core, :, pl.ds(0, HALF)]
        second = buf.at[z, y, core, :, pl.ds(HALF, HALF)]
        row = buf.at[z, :, core, :, pl.ds(0, HALF)]
        col = buf.at[:, y, core, :, pl.ds(HALF, HALF)]
        self.a, self.b = [], []
        for j in range(1, 4):
            py = 8 * z + 2 * ((y + j) % 4) + core
            pz = 8 * ((z + j) % 4) + 2 * y + core
            n = j - 1
            self.a.append(remote(first, first, send.at[n], recv.at[n], py))
            self.a.append(remote(second, second, send.at[n + 3], recv.at[n + 3], pz))
            self.b.append(remote(row, row, send.at[n + 6], recv.at[n + 6], pz))
            self.b.append(remote(col, col, send.at[n + 9], recv.at[n + 9], py))
        half = buf.at[:, :, core]
        self.c = remote(half, half, send.at[12], recv.at[12], sib)

    def start(self):
        for copy in self.a:
            copy.start()

    def middle(self):
        for copy in self.a:
            copy.wait_recv()
        for copy in self.b:
            copy.start()

    def last(self):
        for copy in self.b:
            copy.wait_recv()
        self.c.start()

    def finish(self):
        self.c.wait_recv()
        for copy in self.a + self.b + [self.c]:
            copy.wait_send()


def front_kernel(
    lengths,
    gain,
    cap_in,
    mod,
    video,
    wq,
    wk,
    wv,
    wto_in,
    wqkv,
    heads_out,
    quarter_out,
    enc_out,
    cap,
    wt,
    wto,
    wwin,
    wpad,
    vid,
    tacc,
    mixb,
    s1,
    r1,
    acc,
    s2,
    r2,
    part,
    s3,
    r3,
    w_sem,
    ag_send,
    ag_recv,
    v_send,
    v_recv,
    f_send,
    f_recv,
    r_send,
    r_recv,
    o_sem,
):
    seq, core, chip, y, z = place()
    grp = lax.axis_index("grp")
    sib = seq + 1 - 2 * core
    quarter = seq % 4
    clip = seq // 4
    barrier = pltpu.get_barrier_semaphore()
    greet(sib)

    def greet_one(i, carry):
        greet(2 * ((chip + i) % 16) + core)
        return carry

    lax.fori_loop(1, 16, greet_one, 0)

    loads = [
        pltpu.make_async_copy(wq, wt.at[:, pl.ds(0, 128)], w_sem.at[0]),
        pltpu.make_async_copy(wk, wt.at[:, pl.ds(128, 128)], w_sem.at[1]),
        pltpu.make_async_copy(wv, wt.at[:, pl.ds(256, 128)], w_sem.at[2]),
        pltpu.make_async_copy(wto_in, wto, w_sem.at[3]),
    ]
    base = pl.multiple_of(256 * quarter, 128)
    for n in range(3):
        loads.append(
            pltpu.make_async_copy(
                wqkv.at[:, pl.ds(n * D + base, WIN)], wwin.at[n], w_sem.at[4 + n]
            )
        )
    own_video = pltpu.make_async_copy(video.at[clip], vid.at[seq], w_sem.at[7])
    for copy in loads:
        copy.start()
    own_video.start()

    rows = cap_in[...].astype(F32)
    power = jnp.mean(rows * rows, axis=-1, keepdims=True)
    cap[z, y, core] = (rows * lax.rsqrt(power + 1e-06) * gain[...]).astype(BF)

    pl.semaphore_wait(barrier, 16)
    gather = Gather(cap, ag_send, ag_recv)
    gather.start()

    for copy in loads[4:]:
        copy.wait()
    select = head_select(32 * quarter)
    for n in range(3):
        wpad[:, n * HP : (n + 1) * HP] = jnp.dot(
            wwin[n], select, preferred_element_type=F32
        ).astype(BF)
    gather.middle()

    def send_video(i):
        to = (chip + i) % 16
        return remote(video.at[to // 2], vid.at[seq], v_send.at[i], v_recv.at[i], 2 * to + core)

    def start_video(i, carry):
        send_video(i).start()
        return carry

    lax.fori_loop(1, 16, start_video, 0)
    for copy in loads[:4]:
        copy.wait()
    own_video.wait()
    gather.last()

    row_pos = lax.broadcasted_iota(jnp.int32, (KEYS, KEYS), 0)
    col_pos = lax.broadcasted_iota(jnp.int32, (KEYS, KEYS), 1)
    row_seg = jnp.zeros((KEYS, KEYS), jnp.int32)
    col_seg = jnp.zeros((KEYS, KEYS), jnp.int32)
    end = jnp.int32(0)
    for n in range(8):
        end = end + lengths[grp, n]
        row_seg = row_seg + (row_pos >= end).astype(jnp.int32)
        col_seg = col_seg + (col_pos >= end).astype(jnp.int32)
    same = row_seg == col_seg

    gather.finish()
    tacc[...] = jnp.zeros_like(tacc)

    def project(n, carry):
        at = pl.multiple_of(n * 512, 512)
        left = cap[:, :, :, :, pl.ds(at, 512)].reshape(KEYS, 512)
        tacc[...] += jnp.dot(left, wt[pl.ds(at, 512), :], preferred_element_type=F32)
        return carry

    lax.fori_loop(0, 8, project, 0)
    tquery = tacc[:, 0:128].astype(BF)
    tkey = tacc[:, 128:256].astype(BF)
    tvalue = tacc[:, 256:384].astype(BF)
    lane = lax.broadcasted_iota(jnp.int32, (KEYS, LANE), 1)
    mixes = []
    for n in range(2):
        own = (lane >= n * ET) & (lane < (n + 1) * ET)
        head_query = jnp.where(own, tquery.astype(F32), 0.0).astype(BF)
        score = lax.dot_general(
            head_query, tkey, (((1,), (1,)), ((), ())), preferred_element_type=F32
        )
        score = jnp.where(same, score, -1e30)
        weight = jnp.exp(score - jnp.max(score, axis=-1, keepdims=True))
        total = jnp.sum(weight, axis=-1, keepdims=True)
        mixes.append(jnp.dot(weight.astype(BF), tvalue, preferred_element_type=F32) / total)
    mixed = jnp.where(lane < ET, mixes[0], mixes[1]).astype(BF)
    mixb[...] = mixed.reshape(4, 4, 2, 16, LANE)

    def partial_rows(which, out):
        left = mixb[:, :, which].reshape(256, LANE)

        def one(n, carry):
            at = pl.multiple_of(n * 512, 512)
            value = jnp.dot(left, wto[:, pl.ds(at, 512)], preferred_element_type=F32)
            out[:, :, :, pl.ds(at, 512)] = value.reshape(4, 4, 16, 512).astype(out.dtype)
            return carry

        lax.fori_loop(0, 8, one, 0)

    partial_rows(1 - core, s1)
    pair = remote(s1, r1, r_send.at[0], r_recv.at[0], sib)
    pair.start()
    partial_rows(core, acc)
    pair.wait_recv()

    def add_pair(n, carry):
        at = pl.multiple_of(n * 512, 512)
        value = acc[:, :, :, pl.ds(at, 512)] + r1[:, :, :, pl.ds(at, 512)].astype(F32)
        acc[:, :, :, pl.ds(at, 512)] = value
        s2[:, :, :, pl.ds(at, 512)] = value.astype(BF)
        return carry

    lax.fori_loop(0, 8, add_pair, 0)
    second = []
    for j in range(1, 4):
        ty = (y + j) % 4
        tz = (z + j) % 4
        second.append(
            remote(
                s2.at[:, ty, :, pl.ds(0, HALF)],
                r2.at[0, j - 1],
                r_send.at[j],
                r_recv.at[j],
                8 * z + 2 * ty + core,
            )
        )
        second.append(
            remote(
                s2.at[tz, :, :, pl.ds(HALF, HALF)],
                r2.at[1, j - 1],
                r_send.at[3 + j],
                r_recv.at[3 + j],
                8 * tz + 2 * y + core,
            )
        )
    for copy in second:
        copy.start()

    shift = mod[clip, 0:1, :]
    scale = 1.0 + mod[clip, 1:2, :]
    vlane = lax.broadcasted_iota(jnp.int32, (256, HP), 1) & 127

    def forward(i):
        slot = 2 * ((chip + 16 - i) % 16) + core
        return remote(vid.at[slot], vid.at[slot], f_send.at[i], f_recv.at[i], sib)

    def arrive(i):
        send_video(i).wait_recv()
        forward(i).start()

    def norm(at):
        values = vid[pl.ds(2 * at, 2)].reshape(128, D).astype(F32)
        center = values - jnp.mean(values, axis=-1, keepdims=True)
        spread = jnp.mean(center * center, axis=-1, keepdims=True)
        return (center * lax.rsqrt(spread + 1e-06) * scale + shift).astype(BF)

    forward(0).start()
    arrive(1)

    def project_video(n, carry):
        @pl.when(n < 7)
        def _():
            arrive(2 * n + 2)
            arrive(2 * n + 3)

        forward(2 * n).wait_recv()
        forward(2 * n + 1).wait_recv()
        at0 = (chip + 16 - 2 * n) % 16
        at1 = (chip + 15 - 2 * n) % 16
        normed = jnp.concatenate([norm(at0), norm(at1)], axis=0)
        for which in range(3):
            value = jnp.dot(
                normed, wpad[:, which * HP : (which + 1) * HP], preferred_element_type=F32
            )
            if which == 0:
                value = value * QSCALE
            if which == 2:
                value = jnp.where(vlane == E, 1.0, value)
            value = value.astype(BF)
            for h in range(4):
                piece = value[:, h * LANE : (h + 1) * LANE]
                heads_out[which, h, at0] = piece[:128]
                heads_out[which, h, at1] = piece[128:]
        return carry

    lax.fori_loop(0, 8, project_video, 0)
    keep = pltpu.make_async_copy(vid.at[pl.ds(8 * quarter, 8)], quarter_out, o_sem)
    keep.start()

    for copy in second:
        copy.wait_recv()
    for n in range(4):
        first = acc[n, y, :, 0:HALF]
        other = acc[z, n, :, HALF:DT]
        for j in range(3):
            first = first + r2[0, j, n].astype(F32)
            other = other + r2[1, j, n].astype(F32)
        part[0, n] = first
        part[1, n] = other
        s3[0, n] = first.astype(BF)
        s3[1, n] = other.astype(BF)
    third = []
    for j in range(1, 4):
        ty = (y + j) % 4
        tz = (z + j) % 4
        third.append(
            remote(
                s3.at[0, tz],
                r3.at[0, j - 1],
                r_send.at[6 + j],
                r_recv.at[6 + j],
                8 * tz + 2 * y + core,
            )
        )
        third.append(
            remote(
                s3.at[1, ty],
                r3.at[1, j - 1],
                r_send.at[9 + j],
                r_recv.at[9 + j],
                8 * z + 2 * ty + core,
            )
        )
    for copy in third:
        copy.start()
    for copy in third:
        copy.wait_recv()
    first = part[0, z]
    other = part[1, y]
    for j in range(3):
        first = first + r3[0, j].astype(F32)
        other = other + r3[1, j].astype(F32)
    enc_out[:, 0:HALF] = (cap_in[:, 0:HALF].astype(F32) + first).astype(BF)
    enc_out[:, HALF:DT] = (cap_in[:, HALF:DT].astype(F32) + other).astype(BF)

    keep.wait()
    pair.wait_send()
    for copy in second + third:
        copy.wait_send()

    def drain(i, carry):
        send_video(i).wait_send()
        forward(i).wait_send()
        return carry

    lax.fori_loop(1, 16, drain, 0)
    forward(0).wait_send()


def attend_kernel(
    clip_order,
    enc_in,
    wkv,
    heads,
    win_out,
    kv_out,
    enc,
    mix,
    merge,
    outw,
    ctxf,
    ctx4,
    sel,
    ag_send,
    ag_recv,
    x_send,
    x_recv,
    c_send,
    c_recv,
    p_send,
    p_recv,
    q_send,
    q_recv,
):
    seq, core, chip, y, z = place()
    grp = lax.axis_index("grp")
    sib = seq + 1 - 2 * core
    quarter = seq % 4
    clip = seq // 4
    barrier = pltpu.get_barrier_semaphore()
    greet(sib)
    greet(4 * clip + (quarter + 2) % 4 + 1 - 2 * core)

    def greet_one(i, carry):
        greet(2 * ((chip + i) % 16) + core)
        return carry

    lax.fori_loop(1, 16, greet_one, 0)
    for j in range(1, 4):
        greet((grp + j) % 4, "grp")
    enc[z, y, core] = enc_in[...]
    merge[...] = head_merge(32 * quarter)
    ctxf[...] = jnp.zeros_like(ctxf)
    kv_out[:, :, EP:LANE, :] = jnp.zeros((16, 2, LANE - EP, KEYS), BF)
    pl.semaphore_wait(barrier, 20)

    gather = Gather(enc, ag_send, ag_recv)
    gather.start()

    def cross_x(j):
        mine = ctx4.at[grp]
        return remote(mine, mine, x_send.at[j - 1], x_recv.at[j - 1], (grp + j) % 4, "grp")

    def send_ctx(i):
        to = (chip + i) % 16
        return remote(
            sel.at[to // 2],
            kv_out.at[chip, core, pl.ds(0, EP)],
            c_send.at[i],
            c_recv.at[i],
            2 * to + core,
        )

    own_ctx = pltpu.make_async_copy(
        sel.at[clip], kv_out.at[chip, core, pl.ds(0, EP)], c_send.at[0]
    )
    half = kv_out.at[:, core, pl.ds(0, EP)]
    share = remote(half, half, p_send, p_recv, sib)

    def send_win(j):
        return remote(
            outw.at[j],
            win_out.at[quarter],
            q_send.at[j],
            q_recv.at[j],
            4 * clip + (quarter + j) % 4,
        )

    own_win = pltpu.make_async_copy(outw.at[0], win_out.at[quarter], q_send.at[0])

    def make_context():
        gather.finish()

        def one(n, carry):
            at = pl.multiple_of(n * 512, 512)
            left = enc[:, :, :, :, pl.ds(at, 512)].reshape(KEYS, 512)
            ctxf[:, 0:E] += jnp.dot(left, wkv[pl.ds(at, 512), :], preferred_element_type=F32)
            return carry

        lax.fori_loop(0, 8, one, 0)
        turned = jnp.transpose(ctxf[...])[0:EP, :]
        row = lax.broadcasted_iota(jnp.int32, (EP, KEYS), 0)
        ctx4[grp] = jnp.where(row == E, 1.0, turned).astype(BF)
        for j in range(1, 4):
            cross_x(j).start()

    def spread_context():
        for j in range(1, 4):
            cross_x(j).wait_recv()

        def choose(c, carry):
            def look(i, found):
                return jnp.where(clip_order[i] == grp * 8 + c, i, found)

            caption = lax.fori_loop(0, 32, look, jnp.int32(0))
            sel[c] = ctx4[caption // 8]
            return carry

        lax.fori_loop(0, 8, choose, 0)
        own_ctx.start()

        def one(i, carry):
            send_ctx(i).start()
            return carry

        lax.fori_loop(1, 16, one, 0)

    def share_context():
        own_ctx.wait()

        def one(i, carry):
            send_ctx(i).wait_recv()
            return carry

        lax.fori_loop(1, 16, one, 0)
        share.start()

    def attend(step, carry):
        j = (step // 2 + 1) % 4
        half_at = step % 2
        at = 4 * ((quarter + j) % 4) + 2 * half_at
        for h in range(4):
            query = heads[0, h, pl.ds(at, 2)].reshape(256, LANE)
            key_rows = heads[1, h].reshape(VT, LANE)
            value_rows = heads[2, h].reshape(VT, LANE)
            score = lax.dot_general(
                query, key_rows, (((1,), (1,)), ((), ())), preferred_element_type=F32
            )
            weight = jnp.exp2(score - jnp.max(score, axis=-1, keepdims=True)).astype(BF)
            value = jnp.dot(weight, value_rows, preferred_element_type=F32)
            value = value / value[:, E : E + 1]
            mix[:, h * LANE : (h + 1) * LANE] = value.astype(BF)
        outw[j, pl.ds(pl.multiple_of(256 * half_at, 256), 256)] = jnp.dot(
            mix[...], merge[...], preferred_element_type=F32
        ).astype(BF)

        @pl.when((half_at == 1) & (j > 0))
        def _():
            send_win(j).start()

        @pl.when(step == 0)
        def _():
            gather.middle()

        @pl.when(step == 2)
        def _():
            gather.last()

        @pl.when(step == 3)
        def _():
            make_context()

        @pl.when(step == 4)
        def _():
            spread_context()

        @pl.when(step == 6)
        def _():
            share_context()

        return carry

    lax.fori_loop(0, 8, attend, 0)
    own_win.start()
    own_win.wait()
    for j in range(1, 4):
        send_win(j).wait()
        cross_x(j).wait_send()
    share.wait()

    def drain(i, carry):
        send_ctx(i).wait_send()
        return carry

    lax.fori_loop(1, 16, drain, 0)


def cross_kernel(
    clip_order,
    lengths,
    mod,
    win,
    kv,
    residual,
    wo,
    wcq,
    wco,
    out,
    select,
    merge,
    query,
    heads,
    hidden,
    crossw,
    done,
    s_sem,
    r_sem,
):
    seq, core, chip, y, z = place()
    grp = lax.axis_index("grp")
    quarter = seq % 4
    clip = seq // 4
    barrier = pltpu.get_barrier_semaphore()
    own_here = z == quarter

    def greet_one(i, carry):
        @pl.when(4 * i + z != seq)
        def _():
            greet(4 * i + z)

        return carry

    lax.fori_loop(0, 8, greet_one, 0)
    for n in range(4):
        select[n] = head_select(32 * n)
        merge[n] = head_merge(32 * n)

    def look(i, found):
        return jnp.where(clip_order[i] == grp * 8 + clip, i, found)

    caption = lax.fori_loop(0, 32, look, jnp.int32(0))
    pack = caption // 8
    item = caption % 8
    begin = jnp.int32(0)
    finish = jnp.int32(0)
    for n in range(8):
        size = lengths[pack, n]
        begin = begin + jnp.where(n < item, size, 0)
        finish = finish + jnp.where(n <= item, size, 0)
    gate = mod[clip, 2:3, :]
    pl.semaphore_wait(barrier, jnp.where(own_here, 7, 8))

    def send(b):
        return remote(done.at[b], out.at[clip], s_sem.at[b], r_sem.at[clip], 8 * quarter + b)

    def send_own(b):
        return pltpu.make_async_copy(done.at[b], out.at[clip], s_sem.at[b])

    def rows(n, carry):
        at = pl.multiple_of(256 * n, 256)
        update = jnp.dot(win[0, pl.ds(at, 256)], wo[0:WIN, :], preferred_element_type=F32)
        for i in range(1, 4):
            update = update + jnp.dot(
                win[i, pl.ds(at, 256)], wo[256 * i : 256 * i + WIN, :], preferred_element_type=F32
            )
        base = residual[pl.ds(4 * n, 4)].reshape(256, D).astype(F32)
        hidden[...] = (base + gate * update).astype(BF)
        query[...] = (
            jnp.dot(hidden[...], wcq[...], preferred_element_type=F32) * QSCALE
        ).astype(BF)
        key_at = lax.broadcasted_iota(jnp.int32, (256, KEYS), 1)
        keep = (key_at >= begin) & (key_at < finish)
        for i in range(4):
            heads[i] = jnp.dot(
                query[:, 256 * i : 256 * i + WIN], select[i], preferred_element_type=F32
            ).astype(BF)

        def four(i, carry):
            for h in range(4):
                at_head = 4 * i + h
                key_t = kv[at_head // 2, h % 2]
                value_t = kv[8 + at_head // 2, h % 2]
                score = jnp.dot(
                    heads[i, :, h * LANE : (h + 1) * LANE], key_t, preferred_element_type=F32
                )
                score = jnp.where(keep, score, -1e30)
                weight = jnp.exp2(score - jnp.max(score, axis=-1, keepdims=True)).astype(BF)
                value = lax.dot_general(
                    weight, value_t, (((1,), (1,)), ((), ())), preferred_element_type=F32
                )
                value = value / value[:, E : E + 1]
                crossw[i, :, h * LANE : (h + 1) * LANE] = value.astype(BF)
            return carry

        lax.fori_loop(0, 4, four, 0)
        total = hidden[...].astype(F32)
        for i in range(4):
            window = jnp.dot(crossw[i], merge[i], preferred_element_type=F32).astype(BF)
            total = total + jnp.dot(
                window, wco[256 * i : 256 * i + WIN, :], preferred_element_type=F32
            )
        done[pl.ds(4 * n, 4)] = total.astype(BF).reshape(4, 64, D)
        for i in range(4):
            b = 4 * n + i

            @pl.when(8 * quarter + b == seq)
            def _():
                send_own(b).start()

            @pl.when(8 * quarter + b != seq)
            def _():
                send(b).start()

        return carry

    lax.fori_loop(0, 2, rows, 0)

    def drain(b, carry):
        @pl.when(8 * quarter + b == seq)
        def _():
            send_own(b).wait()

        @pl.when(8 * quarter + b != seq)
        def _():
            send(b).wait_send()

        @pl.when(4 * b + z != seq)
        def _():
            pltpu.make_async_remote_copy(
                src_ref=done.at[0],
                dst_ref=out.at[b],
                send_sem=s_sem.at[0],
                recv_sem=r_sem.at[b],
                device_id={"seq": 4 * b + z},
                device_id_type=MESH,
            ).wait_recv()

        return carry

    lax.fori_loop(0, 8, drain, 0)


def params(number):
    return pltpu.CompilerParams(
        collective_id=number, has_side_effects=True, vmem_limit_bytes=58 * MIB
    )


def per_device(
    captions,
    lengths,
    clip_order,
    t5_gain,
    w_tq,
    w_tk,
    w_tv,
    w_to,
    w_kv,
    video,
    modulation,
    w_qkv,
    w_o,
    w_cq,
    w_co,
):
    vmem = pl.BlockSpec(memory_space=pltpu.VMEM)
    smem = pl.BlockSpec(memory_space=pltpu.SMEM)
    anywhere = pl.BlockSpec(memory_space=pl.ANY)
    dma = pltpu.SemaphoreType.DMA
    heads, quarter_rows, encoded = pl.pallas_call(
        front_kernel,
        out_shape=(
            jax.ShapeDtypeStruct((3, 4, 16, 128, LANE), BF),
            jax.ShapeDtypeStruct((8, 64, D), BF),
            jax.ShapeDtypeStruct((16, DT), BF),
        ),
        in_specs=[smem, vmem, vmem, vmem] + [anywhere] * 6,
        out_specs=(vmem, anywhere, vmem),
        scratch_shapes=[
            pltpu.VMEM((4, 4, 2, 16, DT), BF),
            pltpu.VMEM((DT, 384), BF),
            pltpu.VMEM((128, DT), BF),
            pltpu.VMEM((3, D, WIN), BF),
            pltpu.VMEM((D, 3 * HP), BF),
            pltpu.VMEM((32, 64, D), BF),
            pltpu.VMEM((KEYS, 384), F32),
            pltpu.VMEM((4, 4, 2, 16, LANE), BF),
            pltpu.VMEM((4, 4, 16, DT), BF),
            pltpu.VMEM((4, 4, 16, DT), BF),
            pltpu.VMEM((4, 4, 16, DT), F32),
            pltpu.VMEM((4, 4, 16, DT), BF),
            pltpu.VMEM((2, 3, 4, 16, HALF), BF),
            pltpu.VMEM((2, 4, 16, HALF), F32),
            pltpu.VMEM((2, 4, 16, HALF), BF),
            pltpu.VMEM((2, 3, 16, HALF), BF),
            dma((8,)),
            dma((13,)),
            dma((13,)),
            dma((16,)),
            dma((16,)),
            dma((16,)),
            dma((16,)),
            dma((13,)),
            dma((13,)),
            dma,
        ],
        compiler_params=params(0),
        name="front",
    )(
        lengths,
        t5_gain.reshape(1, DT),
        captions,
        modulation,
        video,
        w_tq,
        w_tk,
        w_tv,
        w_to,
        w_qkv,
    )
    win, kv = pl.pallas_call(
        attend_kernel,
        out_shape=(
            jax.ShapeDtypeStruct((4, 512, WIN), BF),
            jax.ShapeDtypeStruct((16, 2, LANE, KEYS), BF),
        ),
        in_specs=[smem, vmem, vmem, vmem],
        out_specs=(vmem, vmem),
        scratch_shapes=[
            pltpu.VMEM((4, 4, 2, 16, DT), BF),
            pltpu.VMEM((256, HP), BF),
            pltpu.VMEM((HP, WIN), BF),
            pltpu.VMEM((4, 512, WIN), BF),
            pltpu.VMEM((KEYS, LANE), F32),
            pltpu.VMEM((4, EP, KEYS), BF),
            pltpu.VMEM((8, EP, KEYS), BF),
            dma((13,)),
            dma((13,)),
            dma((3,)),
            dma((3,)),
            dma((16,)),
            dma((16,)),
            dma,
            dma,
            dma((4,)),
            dma((4,)),
        ],
        compiler_params=params(1),
        name="attend",
    )(clip_order, encoded, w_kv, heads)
    return pl.pallas_call(
        cross_kernel,
        out_shape=jax.ShapeDtypeStruct((8, 64, D), BF),
        in_specs=[smem, smem] + [vmem] * 7,
        out_specs=anywhere,
        scratch_shapes=[
            pltpu.VMEM((4, WIN, HP), BF),
            pltpu.VMEM((4, HP, WIN), BF),
            pltpu.VMEM((256, D), BF),
            pltpu.VMEM((4, 256, HP), BF),
            pltpu.VMEM((256, D), BF),
            pltpu.VMEM((4, 256, HP), BF),
            pltpu.VMEM((8, 64, D), BF),
            dma((8,)),
            dma((8,)),
        ],
        compiler_params=params(2),
        name="cross",
    )(clip_order, lengths, modulation, win, kv, quarter_rows, w_o, w_cq, w_co)


def solution(mesh):
    in_specs = (
        P(("grp", "seq"), None),
        P(),
        P(),
        P(),
        P(None, "seq"),
        P(None, "seq"),
        P(None, "seq"),
        P("seq", None),
        P(None, "seq"),
        P("grp", "seq", None),
        P("grp", None, None),
        P(),
        P(),
        P(),
        P(),
    )
    out_specs = P("grp", "seq", None)
    return jax.shard_map(
        per_device, mesh=mesh, in_specs=in_specs, out_specs=out_specs, check_vma=False
    )
```

```python
import math

import jax
import jax.numpy as jnp
from jax import lax
from jax.experimental import pallas as pl
from jax.experimental.pallas import tpu as pltpu
from jax.sharding import PartitionSpec as P

ET = 64
D = 1152
H = 16
E = 72
DT = 4096
HALF = DT // 2
LANE = 128
WIN = 384
HP = 4 * LANE
KEYS = 512
EP = 80
VT = 2048
MIB = 1024 * 1024
LOG2E = math.log2(math.e)
QSCALE = E ** (-0.5) * LOG2E
BF = jnp.bfloat16
F32 = jnp.float32
ATTEND_STEPS = ((0, "middle"), (3, "last"), (4, "context"), (5, "spread"))
MESH = pl.DeviceIdType.MESH


def place():
    seq = lax.axis_index("seq")
    core = seq % 2
    chip = seq // 2
    return seq, core, chip, chip % 4, chip // 4


def remote(src, dst, send, recv, peer, axis="seq"):
    return pltpu.make_async_remote_copy(
        src_ref=src,
        dst_ref=dst,
        send_sem=send,
        recv_sem=recv,
        device_id={axis: peer},
        device_id_type=MESH,
    )


def greet(peer, axis="seq"):
    pl.semaphore_signal(
        pltpu.get_barrier_semaphore(), inc=1, device_id={axis: peer}, device_id_type=MESH
    )


def head_select(offset):
    row = lax.broadcasted_iota(jnp.int32, (WIN, HP), 0)
    col = lax.broadcasted_iota(jnp.int32, (WIN, HP), 1)
    head = col >> 7
    lane = col & 127
    hit = (row == offset + head * E + lane) & (lane < E)
    return jnp.where(hit, 1.0, 0.0).astype(BF)


class Gather:
    def __init__(self, buf, send, recv):
        seq, core, chip, y, z = place()
        sib = seq + 1 - 2 * core
        first = buf.at[z, y, core, :, pl.ds(0, HALF)]
        second = buf.at[z, y, core, :, pl.ds(HALF, HALF)]
        row = buf.at[z, :, core, :, pl.ds(0, HALF)]
        col = buf.at[:, y, core, :, pl.ds(HALF, HALF)]
        self.a, self.b = [], []
        self.c = [
            remote(row, row, send.at[12], recv.at[12], sib),
            remote(col, col, send.at[13], recv.at[13], sib),
        ]
        for j in range(1, 4):
            py = 8 * z + 2 * ((y + j) % 4) + core
            pz = 8 * ((z + j) % 4) + 2 * y + core
            n = j - 1
            self.a.append(remote(first, first, send.at[n], recv.at[n], py))
            self.a.append(remote(second, second, send.at[n + 3], recv.at[n + 3], pz))
            self.b.append(remote(row, row, send.at[n + 6], recv.at[n + 6], pz))
            self.b.append(remote(col, col, send.at[n + 9], recv.at[n + 9], py))
            near = buf.at[(z + 4 - j) % 4, :, core, :, pl.ds(0, HALF)]
            side = buf.at[:, (y + 4 - j) % 4, core, :, pl.ds(HALF, HALF)]
            self.c.append(remote(near, near, send.at[13 + j], recv.at[13 + j], sib))
            self.c.append(remote(side, side, send.at[16 + j], recv.at[16 + j], sib))

    def start(self):
        for copy in self.a:
            copy.start()

    def middle(self):
        for copy in self.a:
            copy.wait_recv()
        for copy in self.b:
            copy.start()
        for copy in self.c[:2]:
            copy.start()

    def last(self):
        for copy, onward in zip(self.b, self.c[2:]):
            copy.wait_recv()
            onward.start()

    def finish(self):
        for copy in self.c:
            copy.wait_recv()
        for copy in self.a + self.b + self.c:
            copy.wait_send()


def front_kernel(
    lengths,
    gain,
    cap_in,
    mod,
    video,
    wq,
    wk,
    wv,
    wto_in,
    wqkv,
    heads_out,
    quarter_out,
    enc_out,
    cap,
    wt,
    wto,
    wwin,
    wpad,
    vid,
    tacc,
    mixb,
    s1,
    r1,
    acc,
    s2,
    r2,
    part,
    s3,
    r3,
    w_sem,
    ag_send,
    ag_recv,
    v_send,
    v_recv,
    f_send,
    f_recv,
    r_send,
    r_recv,
    o_sem,
):
    seq, core, chip, y, z = place()
    grp = lax.axis_index("grp")
    sib = seq + 1 - 2 * core
    quarter = seq % 4
    clip = seq // 4
    barrier = pltpu.get_barrier_semaphore()
    greet(sib)

    def greet_one(i, carry):
        greet(2 * ((chip + i) % 16) + core)
        return carry

    lax.fori_loop(1, 16, greet_one, 0)

    loads = [
        pltpu.make_async_copy(wq, wt.at[:, pl.ds(0, 128)], w_sem.at[0]),
        pltpu.make_async_copy(wk, wt.at[:, pl.ds(128, 128)], w_sem.at[1]),
        pltpu.make_async_copy(wv, wt.at[:, pl.ds(256, 128)], w_sem.at[2]),
        pltpu.make_async_copy(wto_in, wto, w_sem.at[3]),
    ]
    base = pl.multiple_of(256 * quarter, 128)
    for n in range(3):
        loads.append(
            pltpu.make_async_copy(
                wqkv.at[:, pl.ds(n * D + base, WIN)], wwin.at[n], w_sem.at[4 + n]
            )
        )
    own_video = pltpu.make_async_copy(video.at[clip], vid.at[seq], w_sem.at[7])
    for copy in loads:
        copy.start()
    own_video.start()

    rows = cap_in[...].astype(F32)
    power = jnp.mean(rows * rows, axis=-1, keepdims=True)
    cap[z, y, core] = (rows * lax.rsqrt(power + 1e-06) * gain[...]).astype(BF)

    pl.semaphore_wait(barrier, 16)
    gather = Gather(cap, ag_send, ag_recv)
    gather.start()

    for copy in loads[4:]:
        copy.wait()
    select = head_select(32 * quarter)
    for n in range(3):
        wpad[:, n * HP : (n + 1) * HP] = jnp.dot(
            wwin[n], select, preferred_element_type=F32
        ).astype(BF)
    gather.middle()

    def send_video(i):
        to = (chip + i) % 16
        return remote(video.at[to // 2], vid.at[seq], v_send.at[i], v_recv.at[i], 2 * to + core)

    def start_video(i, carry):
        send_video(i).start()
        return carry

    lax.fori_loop(1, 16, start_video, 0)
    for copy in loads[:4]:
        copy.wait()
    own_video.wait()
    gather.last()

    row_pos = lax.broadcasted_iota(jnp.int32, (KEYS, KEYS), 0)
    col_pos = lax.broadcasted_iota(jnp.int32, (KEYS, KEYS), 1)
    row_seg = jnp.zeros((KEYS, KEYS), jnp.int32)
    col_seg = jnp.zeros((KEYS, KEYS), jnp.int32)
    end = jnp.int32(0)
    for n in range(8):
        end = end + lengths[grp, n]
        row_seg = row_seg + (row_pos >= end).astype(jnp.int32)
        col_seg = col_seg + (col_pos >= end).astype(jnp.int32)
    same = row_seg == col_seg

    gather.finish()
    tacc[...] = jnp.zeros_like(tacc)

    def project(n, carry):
        at = pl.multiple_of(n * 512, 512)
        left = cap[:, :, :, :, pl.ds(at, 512)].reshape(KEYS, 512)
        tacc[...] += jnp.dot(left, wt[pl.ds(at, 512), :], preferred_element_type=F32)
        return carry

    lax.fori_loop(0, 8, project, 0)
    tquery = tacc[:, 0:128].astype(BF)
    tkey = tacc[:, 128:256].astype(BF)
    tvalue = tacc[:, 256:384].astype(BF)
    lane = lax.broadcasted_iota(jnp.int32, (KEYS, LANE), 1)
    mixes = []
    for n in range(2):
        own = (lane >= n * ET) & (lane < (n + 1) * ET)
        head_query = jnp.where(own, tquery.astype(F32), 0.0).astype(BF)
        score = lax.dot_general(
            head_query, tkey, (((1,), (1,)), ((), ())), preferred_element_type=F32
        )
        score = jnp.where(same, score, -1e30)
        weight = jnp.exp(score - jnp.max(score, axis=-1, keepdims=True))
        total = jnp.sum(weight, axis=-1, keepdims=True)
        mixes.append(jnp.dot(weight.astype(BF), tvalue, preferred_element_type=F32) / total)
    mixed = jnp.where(lane < ET, mixes[0], mixes[1]).astype(BF)
    mixb[...] = mixed.reshape(4, 4, 2, 16, LANE)

    def partial_rows(which, out):
        left = mixb[:, :, which].reshape(256, LANE)

        def one(n, carry):
            at = pl.multiple_of(n * 512, 512)
            value = jnp.dot(left, wto[:, pl.ds(at, 512)], preferred_element_type=F32)
            out[:, :, :, pl.ds(at, 512)] = value.reshape(4, 4, 16, 512).astype(out.dtype)
            return carry

        lax.fori_loop(0, 8, one, 0)

    partial_rows(1 - core, s1)
    pair = remote(s1, r1, r_send.at[0], r_recv.at[0], sib)
    pair.start()
    partial_rows(core, acc)
    pair.wait_recv()

    def add_pair(n, carry):
        at = pl.multiple_of(n * 512, 512)
        value = acc[:, :, :, pl.ds(at, 512)] + r1[:, :, :, pl.ds(at, 512)].astype(F32)
        acc[:, :, :, pl.ds(at, 512)] = value
        s2[:, :, :, pl.ds(at, 512)] = value.astype(BF)
        return carry

    lax.fori_loop(0, 8, add_pair, 0)
    second = []
    for j in range(1, 4):
        ty = (y + j) % 4
        tz = (z + j) % 4
        second.append(
            remote(
                s2.at[:, ty, :, pl.ds(0, HALF)],
                r2.at[0, j - 1],
                r_send.at[j],
                r_recv.at[j],
                8 * z + 2 * ty + core,
            )
        )
        second.append(
            remote(
                s2.at[tz, :, :, pl.ds(HALF, HALF)],
                r2.at[1, j - 1],
                r_send.at[3 + j],
                r_recv.at[3 + j],
                8 * tz + 2 * y + core,
            )
        )
    for copy in second:
        copy.start()

    shift = mod[0, pl.ds(clip, 1), :]
    scale = 1.0 + mod[1, pl.ds(clip, 1), :]
    vlane = lax.broadcasted_iota(jnp.int32, (256, HP), 1) & 127

    def forward(i):
        slot = 2 * ((chip + 16 - i) % 16) + core
        return remote(vid.at[slot], vid.at[slot], f_send.at[i], f_recv.at[i], sib)

    def arrive(i):
        send_video(i).wait_recv()
        forward(i).start()

    def norm(at):
        values = vid[pl.ds(2 * at, 2)].reshape(128, D).astype(F32)
        center = values - jnp.mean(values, axis=-1, keepdims=True)
        spread = jnp.mean(center * center, axis=-1, keepdims=True)
        return (center * lax.rsqrt(spread + 1e-06) * scale + shift).astype(BF)

    forward(0).start()
    arrive(1)

    def project_video(n, carry):
        @pl.when(n < 7)
        def _():
            arrive(2 * n + 2)
            arrive(2 * n + 3)

        forward(2 * n).wait_recv()
        forward(2 * n + 1).wait_recv()
        at0 = (chip + 16 - 2 * n) % 16
        at1 = (chip + 15 - 2 * n) % 16
        normed = jnp.concatenate([norm(at0), norm(at1)], axis=0)
        for which in range(3):
            value = jnp.dot(
                normed, wpad[:, which * HP : (which + 1) * HP], preferred_element_type=F32
            )
            if which == 0:
                value = value * QSCALE
            if which == 2:
                value = jnp.where(vlane == E, 1.0, value)
            value = value.astype(BF)
            for h in range(4):
                piece = value[:, h * LANE : (h + 1) * LANE]
                heads_out[which, h, at0] = piece[:128]
                heads_out[which, h, at1] = piece[128:]
        return carry

    lax.fori_loop(0, 8, project_video, 0)
    keep = pltpu.make_async_copy(vid.at[pl.ds(8 * quarter, 8)], quarter_out, o_sem)
    keep.start()

    for copy in second:
        copy.wait_recv()
    for n in range(4):
        first = acc[n, y, :, 0:HALF]
        other = acc[z, n, :, HALF:DT]
        for j in range(3):
            first = first + r2[0, j, n].astype(F32)
            other = other + r2[1, j, n].astype(F32)
        part[0, n] = first
        part[1, n] = other
        s3[0, n] = first.astype(BF)
        s3[1, n] = other.astype(BF)
    third = []
    for j in range(1, 4):
        ty = (y + j) % 4
        tz = (z + j) % 4
        third.append(
            remote(
                s3.at[0, tz],
                r3.at[0, j - 1],
                r_send.at[6 + j],
                r_recv.at[6 + j],
                8 * tz + 2 * y + core,
            )
        )
        third.append(
            remote(
                s3.at[1, ty],
                r3.at[1, j - 1],
                r_send.at[9 + j],
                r_recv.at[9 + j],
                8 * z + 2 * ty + core,
            )
        )
    for copy in third:
        copy.start()
    for copy in third:
        copy.wait_recv()
    first = part[0, z]
    other = part[1, y]
    for j in range(3):
        first = first + r3[0, j].astype(F32)
        other = other + r3[1, j].astype(F32)
    enc_out[:, 0:HALF] = (cap_in[:, 0:HALF].astype(F32) + first).astype(BF)
    enc_out[:, HALF:DT] = (cap_in[:, HALF:DT].astype(F32) + other).astype(BF)

    keep.wait()
    pair.wait_send()
    for copy in second + third:
        copy.wait_send()

    def drain(i, carry):
        send_video(i).wait_send()
        forward(i).wait_send()
        return carry

    lax.fori_loop(1, 16, drain, 0)
    forward(0).wait_send()


def attend_kernel(
    lengths,
    clip_order,
    enc_in,
    mod,
    wkv,
    heads,
    residual_in,
    wo,
    wcq,
    wco,
    out,
    enc,
    mix,
    outw,
    win,
    ctx4,
    sel,
    kv,
    select,
    query,
    done,
    cross,
    hidden,
    residual,
    wob,
    wcqb,
    wcob,
    w_sem,
    h_send,
    h_recv,
    x_send,
    x_recv,
    c_send,
    c_recv,
    p_send,
    p_recv,
    q_send,
    q_recv,
    o_send,
    o_recv,
):
    seq, core, chip, y, z = place()
    grp = lax.axis_index("grp")
    sib = seq + 1 - 2 * core
    quarter = seq % 4
    clip = seq // 4
    barrier = pltpu.get_barrier_semaphore()

    def greet_one(i, carry):
        greet((seq + i) % 32)
        return carry

    lax.fori_loop(1, 32, greet_one, 0)
    for j in range(1, 4):
        greet((grp + j) % 4, "grp")
    enc[z, y, core] = enc_in[...]
    kv[:, :, EP:LANE, :] = jnp.zeros((16, 2, LANE - EP, KEYS), BF)
    pl.semaphore_wait(barrier, 34)
    again = Gather(enc, h_send, h_recv)
    again.start()
    loads = [
        pltpu.make_async_copy(wo.at[:, pl.ds(n * WIN, WIN)], wob.at[n], w_sem.at[n])
        for n in range(3)
    ]
    for n in range(3):
        loads.append(
            pltpu.make_async_copy(wcq.at[:, pl.ds(n * WIN, WIN)], wcqb.at[n], w_sem.at[3 + n])
        )
    loads.append(pltpu.make_async_copy(wco, wcob, w_sem.at[6]))
    loads.append(pltpu.make_async_copy(residual_in, residual, w_sem.at[7]))
    for copy in loads:
        copy.start()
    for n in range(4):
        select[n] = head_select(32 * n)
    gate = mod[2, pl.ds(clip, 1), :]

    def cross_x(j):
        mine = ctx4.at[grp]
        return remote(mine, mine, x_send.at[j - 1], x_recv.at[j - 1], (grp + j) % 4, "grp")

    def send_ctx(i):
        to = (chip + i) % 16
        return remote(
            sel.at[to // 2],
            kv.at[chip, core, pl.ds(0, EP)],
            c_send.at[i],
            c_recv.at[i],
            2 * to + core,
        )

    own_ctx = pltpu.make_async_copy(sel.at[clip], kv.at[chip, core, pl.ds(0, EP)], c_send.at[0])
    half = kv.at[:, core, pl.ds(0, EP)]
    share = remote(half, half, p_send, p_recv, sib)

    def make_context():
        again.finish()

        def one(n, total):
            at = pl.multiple_of(n * 512, 512)
            left = enc[:, :, :, :, pl.ds(at, 512)].reshape(KEYS, 512)
            return total + lax.dot_general(
                wkv[:, pl.ds(at, 512)],
                left,
                (((1,), (1,)), ((), ())),
                preferred_element_type=F32,
            )

        turned = lax.fori_loop(0, 8, one, jnp.zeros((E, KEYS), F32))
        tail = lax.broadcasted_iota(jnp.int32, (EP - E, KEYS), 0)
        tail = jnp.where(tail == 0, 1.0, 0.0)
        ctx4[grp] = jnp.concatenate([turned, tail], axis=0).astype(BF)
        for j in range(1, 4):
            cross_x(j).start()

    def spread_context():
        for j in range(1, 4):
            cross_x(j).wait_recv()

        def choose(c, carry):
            def look(i, found):
                return jnp.where(clip_order[i] == grp * 8 + c, i, found)

            caption = lax.fori_loop(0, 32, look, jnp.int32(0))
            sel[c] = ctx4[caption // 8]
            return carry

        lax.fori_loop(0, 8, choose, 0)
        own_ctx.start()

        def one(i, carry):
            send_ctx(i).start()
            return carry

        lax.fori_loop(1, 16, one, 0)

    def share_context():
        own_ctx.wait()

        def one(i, carry):
            send_ctx(i).wait_recv()
            return carry

        lax.fori_loop(1, 16, one, 0)
        share.start()

    def at_step(step, when, work):
        @pl.when(step == when)
        def _():
            work()

    locals_of = {
        "middle": again.middle,
        "last": again.last,
        "context": make_context,
        "spread": spread_context,
    }

    def send_win(j):
        to = 4 * clip + (quarter + j) % 4
        return remote(outw.at[j], win.at[quarter], q_send.at[j], q_recv.at[j], to)

    own_win = pltpu.make_async_copy(outw.at[0], win.at[quarter], q_send.at[0])

    def attend(step, carry):
        j = (step // 2 + 1) % 4
        at = 4 * ((quarter + j) % 4)
        for u in range(2):
            h = 2 * (step % 2) + u
            q_rows = heads[0, h, pl.ds(at, 4)].reshape(512, LANE)
            key_rows = heads[1, h].reshape(VT, LANE)
            value_rows = heads[2, h].reshape(VT, LANE)
            score = lax.dot_general(
                q_rows, key_rows, (((1,), (1,)), ((), ())), preferred_element_type=F32
            )
            weight = jnp.exp2(score - jnp.max(score, axis=-1, keepdims=True)).astype(BF)
            value = jnp.dot(weight, value_rows, preferred_element_type=F32)
            value = value / value[:, E : E + 1]
            mix[h] = value.astype(BF)

        @pl.when(step % 2 == 1)
        def _():
            flat = jnp.concatenate([mix[h] for h in range(4)], axis=1)
            outw[j] = lax.dot_general(
                flat, select[quarter], (((1,), (1,)), ((), ())), preferred_element_type=F32
            ).astype(BF)

        @pl.when((step % 2 == 1) & (j > 0))
        def _():
            send_win(j).start()

        for when, work in ATTEND_STEPS:
            at_step(step, when, locals_of[work])
        return carry

    lax.fori_loop(0, 8, attend, 0)
    own_win.start()

    def look(i, found):
        return jnp.where(clip_order[i] == grp * 8 + clip, i, found)

    caption = lax.fori_loop(0, 32, look, jnp.int32(0))
    pack = caption // 8
    item = caption % 8
    begin = jnp.int32(0)
    finish = jnp.int32(0)
    for n in range(8):
        size = lengths[pack, n]
        begin = begin + jnp.where(n < item, size, 0)
        finish = finish + jnp.where(n <= item, size, 0)
    for copy in loads:
        copy.wait()
    own_win.wait()
    for j in range(1, 4):
        send_win(j).wait()

    def before(n, carry):
        at = pl.multiple_of(256 * n, 256)
        for c in range(3):
            cols = slice(c * WIN, (c + 1) * WIN)
            update = jnp.dot(
                win[0, pl.ds(at, 256)], wob[c, 0:WIN], preferred_element_type=F32
            )
            for i in range(1, 4):
                update = update + jnp.dot(
                    win[i, pl.ds(at, 256)],
                    wob[c, 256 * i : 256 * i + WIN],
                    preferred_element_type=F32,
                )
            first_rows = residual[pl.ds(4 * n, 4), :, cols].reshape(256, WIN)
            hidden[pl.ds(at, 256), cols] = (
                first_rows.astype(F32) + gate[:, cols] * update
            ).astype(BF)
        for c in range(3):
            value = jnp.dot(
                hidden[pl.ds(at, 256)], wcqb[c], preferred_element_type=F32
            )
            query[pl.ds(4 * n, 4), :, c * WIN : (c + 1) * WIN] = (
                (value * QSCALE).astype(BF).reshape(4, 64, WIN)
            )
        for i in range(4):
            cross[i, pl.ds(at, 256)] = jnp.dot(
                query[pl.ds(4 * n, 4), :, 256 * i : 256 * i + WIN].reshape(256, WIN),
                select[i],
                preferred_element_type=F32,
            ).astype(BF)
        return carry

    lax.fori_loop(0, 2, before, 0)
    share_context()
    share.wait()

    def send(b):
        return remote(done.at[b], out.at[clip], o_send.at[b], o_recv.at[clip], 8 * quarter + b)

    def send_own(b):
        return pltpu.make_async_copy(done.at[b], out.at[clip], o_send.at[b])

    key_at = lax.broadcasted_iota(jnp.int32, (256, KEYS), 1)
    keep = (key_at >= begin) & (key_at < finish)

    def after(n, carry):
        at = pl.multiple_of(256 * n, 256)

        def four(i, carry):
            for h in range(4):
                at_head = 2 * i + h // 2
                lanes = slice(h * LANE, (h + 1) * LANE)
                score = jnp.dot(
                    cross[i, pl.ds(at, 256), lanes],
                    kv[at_head, h % 2],
                    preferred_element_type=F32,
                )
                score = jnp.where(keep, score, -1e30)
                weight = jnp.exp2(score - jnp.max(score, axis=-1, keepdims=True)).astype(BF)
                value = lax.dot_general(
                    weight,
                    kv[8 + at_head, h % 2],
                    (((1,), (1,)), ((), ())),
                    preferred_element_type=F32,
                )
                value = value / value[:, E : E + 1]
                cross[i, pl.ds(at, 256), lanes] = value.astype(BF)
            return carry

        lax.fori_loop(0, 4, four, 0)
        total = hidden[pl.ds(at, 256)].astype(F32)
        for i in range(4):
            window = lax.dot_general(
                cross[i, pl.ds(at, 256)],
                select[i],
                (((1,), (1,)), ((), ())),
                preferred_element_type=F32,
            ).astype(BF)
            total = total + jnp.dot(
                window, wcob[256 * i : 256 * i + WIN], preferred_element_type=F32
            )
        done[pl.ds(4 * n, 4)] = total.astype(BF).reshape(4, 64, D)
        for i in range(4):
            b = 4 * n + i

            @pl.when(8 * quarter + b == seq)
            def _():
                send_own(b).start()

            @pl.when(8 * quarter + b != seq)
            def _():
                send(b).start()

        return carry

    lax.fori_loop(0, 2, after, 0)

    for j in range(1, 4):
        cross_x(j).wait_send()

    def drain(i, carry):
        send_ctx(i).wait_send()
        return carry

    lax.fori_loop(1, 16, drain, 0)

    def drain_out(b, carry):
        @pl.when(8 * quarter + b == seq)
        def _():
            send_own(b).wait()

        @pl.when(8 * quarter + b != seq)
        def _():
            send(b).wait_send()

        @pl.when(4 * b + z != seq)
        def _():
            remote(done.at[0], out.at[b], o_send.at[0], o_recv.at[b], 4 * b + z).wait_recv()

        return carry

    lax.fori_loop(0, 8, drain_out, 0)


def params(number):
    return pltpu.CompilerParams(
        collective_id=number, has_side_effects=True, vmem_limit_bytes=58 * MIB
    )


def per_device(
    captions,
    lengths,
    clip_order,
    t5_gain,
    w_tq,
    w_tk,
    w_tv,
    w_to,
    w_kv,
    video,
    modulation,
    w_qkv,
    w_o,
    w_cq,
    w_co,
):
    vmem = pl.BlockSpec(memory_space=pltpu.VMEM)
    smem = pl.BlockSpec(memory_space=pltpu.SMEM)
    anywhere = pl.BlockSpec(memory_space=pl.ANY)
    dma = pltpu.SemaphoreType.DMA
    mods = jnp.transpose(modulation, (1, 0, 2))
    heads, quarter_rows, encoded = pl.pallas_call(
        front_kernel,
        out_shape=(
            jax.ShapeDtypeStruct((3, 4, 16, 128, LANE), BF),
            jax.ShapeDtypeStruct((8, 64, D), BF),
            jax.ShapeDtypeStruct((16, DT), BF),
        ),
        in_specs=[smem, vmem, vmem, vmem] + [anywhere] * 6,
        out_specs=(vmem, anywhere, vmem),
        scratch_shapes=[
            pltpu.VMEM((4, 4, 2, 16, DT), BF),
            pltpu.VMEM((DT, 384), BF),
            pltpu.VMEM((128, DT), BF),
            pltpu.VMEM((3, D, WIN), BF),
            pltpu.VMEM((D, 3 * HP), BF),
            pltpu.VMEM((32, 64, D), BF),
            pltpu.VMEM((KEYS, 384), F32),
            pltpu.VMEM((4, 4, 2, 16, LANE), BF),
            pltpu.VMEM((4, 4, 16, DT), BF),
            pltpu.VMEM((4, 4, 16, DT), BF),
            pltpu.VMEM((4, 4, 16, DT), F32),
            pltpu.VMEM((4, 4, 16, DT), BF),
            pltpu.VMEM((2, 3, 4, 16, HALF), BF),
            pltpu.VMEM((2, 4, 16, HALF), F32),
            pltpu.VMEM((2, 4, 16, HALF), BF),
            pltpu.VMEM((2, 3, 16, HALF), BF),
            dma((8,)),
            dma((20,)),
            dma((20,)),
            dma((16,)),
            dma((16,)),
            dma((16,)),
            dma((16,)),
            dma((13,)),
            dma((13,)),
            dma,
        ],
        compiler_params=params(0),
        name="front",
    )(
        lengths,
        t5_gain.reshape(1, DT),
        captions,
        mods,
        video,
        w_tq,
        w_tk,
        w_tv,
        w_to,
        w_qkv,
    )
    counts = (8, 20, 20, 3, 3, 16, 16, 0, 0, 4, 4, 8, 8)
    return pl.pallas_call(
        attend_kernel,
        out_shape=jax.ShapeDtypeStruct((8, 64, D), BF),
        in_specs=[smem, smem, vmem, vmem, vmem, vmem] + [anywhere] * 4,
        out_specs=anywhere,
        scratch_shapes=[
            pltpu.VMEM((4, 4, 2, 16, DT), BF),
            pltpu.VMEM((4, 512, LANE), BF),
            pltpu.VMEM((4, 512, WIN), BF),
            pltpu.VMEM((4, 512, WIN), BF),
            pltpu.VMEM((4, EP, KEYS), BF),
            pltpu.VMEM((8, EP, KEYS), BF),
            pltpu.VMEM((16, 2, LANE, KEYS), BF),
            pltpu.VMEM((4, WIN, HP), BF),
            pltpu.VMEM((8, 64, D), BF),
            pltpu.VMEM((8, 64, D), BF),
            pltpu.VMEM((4, 512, HP), BF),
            pltpu.VMEM((512, D), BF),
            pltpu.VMEM((8, 64, D), BF),
            pltpu.VMEM((3, D, WIN), BF),
            pltpu.VMEM((3, D, WIN), BF),
            pltpu.VMEM((D, D), BF),
        ]
        + [dma((n,)) if n else dma for n in counts],
        compiler_params=params(1),
        name="attend",
    )(
        lengths,
        clip_order,
        encoded,
        mods,
        w_kv.T,
        heads,
        quarter_rows,
        w_o,
        w_cq,
        w_co,
    )


def solution(mesh):
    in_specs = (
        P(("grp", "seq"), None),
        P(),
        P(),
        P(),
        P(None, "seq"),
        P(None, "seq"),
        P(None, "seq"),
        P("seq", None),
        P(None, "seq"),
        P("grp", "seq", None),
        P("grp", None, None),
        P(),
        P(),
        P(),
        P(),
    )
    out_specs = P("grp", "seq", None)
    return jax.shard_map(
        per_device, mesh=mesh, in_specs=in_specs, out_specs=out_specs, check_vma=False
    )
```

```python
import math

import jax
import jax.numpy as jnp
from jax import lax
from jax.experimental import pallas as pl
from jax.experimental.pallas import tpu as pltpu
from jax.sharding import PartitionSpec as P

ET = 64
D = 1152
H = 16
E = 72
DT = 4096
HALF = DT // 2
LANE = 128
WIN = 384
HP = 4 * LANE
KEYS = 512
EP = 80
VT = 2048
MIB = 1024 * 1024
LOG2E = math.log2(math.e)
QSCALE = E ** (-0.5) * LOG2E
BF = jnp.bfloat16
F32 = jnp.float32
ATTEND_STEPS = ((0, "middle"), (3, "last"), (3, "context"), (4, "spread"))
MESH = pl.DeviceIdType.MESH


def place():
    seq = lax.axis_index("seq")
    core = seq % 2
    chip = seq // 2
    return seq, core, chip, chip % 4, chip // 4


def remote(src, dst, send, recv, peer, axis="seq"):
    return pltpu.make_async_remote_copy(
        src_ref=src,
        dst_ref=dst,
        send_sem=send,
        recv_sem=recv,
        device_id={axis: peer},
        device_id_type=MESH,
    )


def greet(peer, axis="seq"):
    pl.semaphore_signal(
        pltpu.get_barrier_semaphore(), inc=1, device_id={axis: peer}, device_id_type=MESH
    )


def head_select(offset):
    row = lax.broadcasted_iota(jnp.int32, (WIN, HP), 0)
    col = lax.broadcasted_iota(jnp.int32, (WIN, HP), 1)
    head = col >> 7
    lane = col & 127
    hit = (row == offset + head * E + lane) & (lane < E)
    return jnp.where(hit, 1.0, 0.0).astype(BF)


class Gather:
    def __init__(self, buf, send, recv):
        seq, core, chip, y, z = place()
        sib = seq + 1 - 2 * core
        first = buf.at[z, y, core, :, pl.ds(0, HALF)]
        second = buf.at[z, y, core, :, pl.ds(HALF, HALF)]
        row = buf.at[z, :, core, :, pl.ds(0, HALF)]
        col = buf.at[:, y, core, :, pl.ds(HALF, HALF)]
        self.a, self.b = [], []
        self.c = [
            remote(row, row, send.at[12], recv.at[12], sib),
            remote(col, col, send.at[13], recv.at[13], sib),
        ]
        for j in range(1, 4):
            py = 8 * z + 2 * ((y + j) % 4) + core
            pz = 8 * ((z + j) % 4) + 2 * y + core
            n = j - 1
            self.a.append(remote(first, first, send.at[n], recv.at[n], py))
            self.a.append(remote(second, second, send.at[n + 3], recv.at[n + 3], pz))
            self.b.append(remote(row, row, send.at[n + 6], recv.at[n + 6], pz))
            self.b.append(remote(col, col, send.at[n + 9], recv.at[n + 9], py))
            near = buf.at[(z + 4 - j) % 4, :, core, :, pl.ds(0, HALF)]
            side = buf.at[:, (y + 4 - j) % 4, core, :, pl.ds(HALF, HALF)]
            self.c.append(remote(near, near, send.at[13 + j], recv.at[13 + j], sib))
            self.c.append(remote(side, side, send.at[16 + j], recv.at[16 + j], sib))

    def start(self):
        for copy in self.a:
            copy.start()

    def middle(self):
        for copy in self.a:
            copy.wait_recv()
        for copy in self.b:
            copy.start()
        for copy in self.c[:2]:
            copy.start()

    def last(self):
        for copy, onward in zip(self.b, self.c[2:]):
            copy.wait_recv()
            onward.start()

    def finish(self):
        for copy in self.c:
            copy.wait_recv()
        for copy in self.a + self.b + self.c:
            copy.wait_send()


def front_kernel(
    lengths,
    gain,
    cap_in,
    mod,
    video,
    wq,
    wk,
    wv,
    wto_in,
    wqkv,
    heads_out,
    quarter_out,
    enc_out,
    heads,
    cap,
    wt,
    wto,
    wwin,
    wpad,
    vid,
    tacc,
    mixb,
    s1,
    r1,
    acc,
    s2,
    r2,
    part,
    s3,
    r3,
    w_sem,
    ag_send,
    ag_recv,
    v_send,
    v_recv,
    f_send,
    f_recv,
    r_send,
    r_recv,
    o_sem,
    k_sem,
):
    seq, core, chip, y, z = place()
    grp = lax.axis_index("grp")
    sib = seq + 1 - 2 * core
    quarter = seq % 4
    clip = seq // 4
    barrier = pltpu.get_barrier_semaphore()
    greet(sib)

    def greet_one(i, carry):
        greet(2 * ((chip + i) % 16) + core)
        return carry

    lax.fori_loop(1, 16, greet_one, 0)

    loads = [
        pltpu.make_async_copy(wq, wt.at[:, pl.ds(0, 128)], w_sem.at[0]),
        pltpu.make_async_copy(wk, wt.at[:, pl.ds(128, 128)], w_sem.at[1]),
        pltpu.make_async_copy(wv, wt.at[:, pl.ds(256, 128)], w_sem.at[2]),
        pltpu.make_async_copy(wto_in, wto, w_sem.at[3]),
    ]
    base = pl.multiple_of(256 * quarter, 128)
    for n in range(3):
        loads.append(
            pltpu.make_async_copy(
                wqkv.at[:, pl.ds(n * D + base, WIN)], wwin.at[n], w_sem.at[4 + n]
            )
        )
    own_video = pltpu.make_async_copy(video.at[clip], vid.at[seq], w_sem.at[7])
    for copy in loads:
        copy.start()
    own_video.start()

    rows = cap_in[...].astype(F32)
    power = jnp.mean(rows * rows, axis=-1, keepdims=True)
    cap[z, y, core] = (rows * lax.rsqrt(power + 1e-06) * gain[...]).astype(BF)

    pl.semaphore_wait(barrier, 16)
    gather = Gather(cap, ag_send, ag_recv)
    gather.start()

    for copy in loads[4:]:
        copy.wait()
    select = head_select(32 * quarter)
    for n in range(3):
        wpad[:, n * HP : (n + 1) * HP] = jnp.dot(
            wwin[n], select, preferred_element_type=F32
        ).astype(BF)
    gather.middle()

    def send_video(i):
        to = (chip + i) % 16
        return remote(video.at[to // 2], vid.at[seq], v_send.at[i], v_recv.at[i], 2 * to + core)

    def start_video(i, carry):
        send_video(i).start()
        return carry

    lax.fori_loop(1, 16, start_video, 0)
    for copy in loads[:4]:
        copy.wait()
    own_video.wait()
    gather.last()

    row_pos = lax.broadcasted_iota(jnp.int32, (KEYS, KEYS), 0)
    col_pos = lax.broadcasted_iota(jnp.int32, (KEYS, KEYS), 1)
    row_seg = jnp.zeros((KEYS, KEYS), jnp.int32)
    col_seg = jnp.zeros((KEYS, KEYS), jnp.int32)
    end = jnp.int32(0)
    for n in range(8):
        end = end + lengths[grp, n]
        row_seg = row_seg + (row_pos >= end).astype(jnp.int32)
        col_seg = col_seg + (col_pos >= end).astype(jnp.int32)
    same = row_seg == col_seg

    gather.finish()
    tacc[...] = jnp.zeros_like(tacc)

    def project(n, carry):
        at = pl.multiple_of(n * 512, 512)
        left = cap[:, :, :, :, pl.ds(at, 512)].reshape(KEYS, 512)
        tacc[...] += jnp.dot(left, wt[pl.ds(at, 512), :], preferred_element_type=F32)
        return carry

    lax.fori_loop(0, 8, project, 0)
    tquery = tacc[:, 0:128].astype(BF)
    tkey = tacc[:, 128:256].astype(BF)
    tvalue = tacc[:, 256:384].astype(BF)
    lane = lax.broadcasted_iota(jnp.int32, (KEYS, LANE), 1)
    mixes = []
    for n in range(2):
        own = (lane >= n * ET) & (lane < (n + 1) * ET)
        head_query = jnp.where(own, tquery.astype(F32), 0.0).astype(BF)
        score = lax.dot_general(
            head_query, tkey, (((1,), (1,)), ((), ())), preferred_element_type=F32
        )
        score = jnp.where(same, score, -1e30)
        weight = jnp.exp(score - jnp.max(score, axis=-1, keepdims=True))
        total = jnp.sum(weight, axis=-1, keepdims=True)
        mixes.append(jnp.dot(weight.astype(BF), tvalue, preferred_element_type=F32) / total)
    mixed = jnp.where(lane < ET, mixes[0], mixes[1]).astype(BF)
    mixb[...] = mixed.reshape(4, 4, 2, 16, LANE)

    def partial_rows(which, out):
        left = mixb[:, :, which].reshape(256, LANE)

        def one(n, carry):
            at = pl.multiple_of(n * 512, 512)
            value = jnp.dot(left, wto[:, pl.ds(at, 512)], preferred_element_type=F32)
            out[:, :, :, pl.ds(at, 512)] = value.reshape(4, 4, 16, 512).astype(out.dtype)
            return carry

        lax.fori_loop(0, 8, one, 0)

    partial_rows(1 - core, s1)
    pair = remote(s1, r1, r_send.at[0], r_recv.at[0], sib)
    pair.start()
    partial_rows(core, acc)
    pair.wait_recv()

    def add_pair(n, carry):
        at = pl.multiple_of(n * 512, 512)
        value = acc[:, :, :, pl.ds(at, 512)] + r1[:, :, :, pl.ds(at, 512)].astype(F32)
        acc[:, :, :, pl.ds(at, 512)] = value
        s2[:, :, :, pl.ds(at, 512)] = value.astype(BF)
        return carry

    lax.fori_loop(0, 8, add_pair, 0)
    second = []
    for j in range(1, 4):
        ty = (y + j) % 4
        tz = (z + j) % 4
        second.append(
            remote(
                s2.at[:, ty, :, pl.ds(0, HALF)],
                r2.at[0, j - 1],
                r_send.at[j],
                r_recv.at[j],
                8 * z + 2 * ty + core,
            )
        )
        second.append(
            remote(
                s2.at[tz, :, :, pl.ds(HALF, HALF)],
                r2.at[1, j - 1],
                r_send.at[3 + j],
                r_recv.at[3 + j],
                8 * tz + 2 * y + core,
            )
        )
    for copy in second:
        copy.start()

    shift = mod[0, pl.ds(clip, 1), :]
    scale = 1.0 + mod[1, pl.ds(clip, 1), :]
    vlane = lax.broadcasted_iota(jnp.int32, (256, HP), 1) & 127

    def forward(i):
        slot = 2 * ((chip + 16 - i) % 16) + core
        return remote(vid.at[slot], vid.at[slot], f_send.at[i], f_recv.at[i], sib)

    def arrive(i):
        send_video(i).wait_recv()
        forward(i).start()

    def norm(at):
        values = vid[pl.ds(2 * at, 2)].reshape(128, D).astype(F32)
        center = values - jnp.mean(values, axis=-1, keepdims=True)
        spread = jnp.mean(center * center, axis=-1, keepdims=True)
        return (center * lax.rsqrt(spread + 1e-06) * scale + shift).astype(BF)

    forward(0).start()
    arrive(1)

    def keep_heads(i):
        at = (chip + 16 - i) % 16
        return pltpu.make_async_copy(heads.at[:, :, at], heads_out.at[:, :, at], k_sem.at[i])

    def project_video(n, carry):
        @pl.when(n < 7)
        def _():
            arrive(2 * n + 2)
            arrive(2 * n + 3)

        forward(2 * n).wait_recv()
        forward(2 * n + 1).wait_recv()
        at0 = (chip + 16 - 2 * n) % 16
        at1 = (chip + 15 - 2 * n) % 16
        normed = jnp.concatenate([norm(at0), norm(at1)], axis=0)
        for which in range(3):
            value = jnp.dot(
                normed, wpad[:, which * HP : (which + 1) * HP], preferred_element_type=F32
            )
            if which == 0:
                value = value * QSCALE
            if which == 2:
                value = jnp.where(vlane == E, 1.0, value)
            value = value.astype(BF)
            for h in range(4):
                piece = value[:, h * LANE : (h + 1) * LANE]
                heads[which, h, at0] = piece[:128]
                heads[which, h, at1] = piece[128:]
        keep_heads(2 * n).start()
        keep_heads(2 * n + 1).start()
        return carry

    lax.fori_loop(0, 8, project_video, 0)
    keep = pltpu.make_async_copy(vid.at[pl.ds(8 * quarter, 8)], quarter_out, o_sem)
    keep.start()

    for copy in second:
        copy.wait_recv()
    for n in range(4):
        first = acc[n, y, :, 0:HALF]
        other = acc[z, n, :, HALF:DT]
        for j in range(3):
            first = first + r2[0, j, n].astype(F32)
            other = other + r2[1, j, n].astype(F32)
        part[0, n] = first
        part[1, n] = other
        s3[0, n] = first.astype(BF)
        s3[1, n] = other.astype(BF)
    third = []
    for j in range(1, 4):
        ty = (y + j) % 4
        tz = (z + j) % 4
        third.append(
            remote(
                s3.at[0, tz],
                r3.at[0, j - 1],
                r_send.at[6 + j],
                r_recv.at[6 + j],
                8 * tz + 2 * y + core,
            )
        )
        third.append(
            remote(
                s3.at[1, ty],
                r3.at[1, j - 1],
                r_send.at[9 + j],
                r_recv.at[9 + j],
                8 * z + 2 * ty + core,
            )
        )
    for copy in third:
        copy.start()
    for copy in third:
        copy.wait_recv()
    first = part[0, z]
    other = part[1, y]
    for j in range(3):
        first = first + r3[0, j].astype(F32)
        other = other + r3[1, j].astype(F32)
    enc_out[:, 0:HALF] = (cap_in[:, 0:HALF].astype(F32) + first).astype(BF)
    enc_out[:, HALF:DT] = (cap_in[:, HALF:DT].astype(F32) + other).astype(BF)

    keep.wait()
    pair.wait_send()
    for copy in second + third:
        copy.wait_send()

    def drain(i, carry):
        send_video(i).wait_send()
        forward(i).wait_send()
        return carry

    lax.fori_loop(1, 16, drain, 0)
    forward(0).wait_send()

    def drain_heads(i, carry):
        keep_heads(i).wait()
        return carry

    lax.fori_loop(0, 16, drain_heads, 0)


def attend_kernel(
    lengths,
    clip_order,
    enc_in,
    mod,
    wkv,
    heads_in,
    residual_in,
    wo,
    wcq,
    wco,
    out,
    heads,
    enc,
    mix,
    outw,
    win,
    ctx4,
    sel,
    kv,
    select,
    query,
    done,
    cross,
    hidden,
    residual,
    wob,
    wcqb,
    wcob,
    w_sem,
    h_send,
    h_recv,
    x_send,
    x_recv,
    c_send,
    c_recv,
    p_send,
    p_recv,
    q_send,
    q_recv,
    o_send,
    o_recv,
):
    seq, core, chip, y, z = place()
    grp = lax.axis_index("grp")
    sib = seq + 1 - 2 * core
    quarter = seq % 4
    clip = seq // 4
    barrier = pltpu.get_barrier_semaphore()

    heads_load = pltpu.make_async_copy(heads_in, heads, w_sem.at[8])
    heads_load.start()

    def greet_one(i, carry):
        greet((seq + i) % 32)
        return carry

    lax.fori_loop(1, 32, greet_one, 0)
    for j in range(1, 4):
        greet((grp + j) % 4, "grp")
    enc[z, y, core] = enc_in[...]
    kv[:, :, EP:LANE, :] = jnp.zeros((16, 2, LANE - EP, KEYS), BF)
    captions = [jnp.int32(0)] * 8
    for i in range(32):
        which = clip_order[i] - grp * 8
        captions = [jnp.where(which == c, i, found) for c, found in enumerate(captions)]
    pl.semaphore_wait(barrier, 34)
    again = Gather(enc, h_send, h_recv)
    again.start()
    loads = [
        pltpu.make_async_copy(wo.at[:, pl.ds(n * WIN, WIN)], wob.at[n], w_sem.at[n])
        for n in range(3)
    ]
    for n in range(3):
        loads.append(
            pltpu.make_async_copy(wcq.at[:, pl.ds(n * WIN, WIN)], wcqb.at[n], w_sem.at[3 + n])
        )
    loads.append(pltpu.make_async_copy(wco, wcob, w_sem.at[6]))
    loads.append(pltpu.make_async_copy(residual_in, residual, w_sem.at[7]))
    for copy in loads:
        copy.start()
    for n in range(4):
        select[n] = head_select(32 * n)
    gate = mod[2, pl.ds(clip, 1), :]

    def cross_x(j):
        mine = ctx4.at[grp]
        return remote(mine, mine, x_send.at[j - 1], x_recv.at[j - 1], (grp + j) % 4, "grp")

    def send_ctx(i):
        to = (chip + i) % 16
        return remote(
            sel.at[to // 2],
            kv.at[chip, core, pl.ds(0, EP)],
            c_send.at[i],
            c_recv.at[i],
            2 * to + core,
        )

    own_ctx = pltpu.make_async_copy(sel.at[clip], kv.at[chip, core, pl.ds(0, EP)], c_send.at[0])

    def share(i):
        rows = kv.at[(chip + 16 - i) % 16, core, pl.ds(0, EP)]
        return remote(rows, rows, p_send.at[i], p_recv.at[i], sib)

    def make_context():
        again.finish()

        def one(n, total):
            at = pl.multiple_of(n * 512, 512)
            left = enc[:, :, :, :, pl.ds(at, 512)].reshape(KEYS, 512)
            return total + lax.dot_general(
                wkv[:, pl.ds(at, 512)],
                left,
                (((1,), (1,)), ((), ())),
                preferred_element_type=F32,
            )

        turned = lax.fori_loop(0, 8, one, jnp.zeros((E, KEYS), F32))
        tail = lax.broadcasted_iota(jnp.int32, (EP - E, KEYS), 0)
        tail = jnp.where(tail == 0, 1.0, 0.0)
        ctx4[grp] = jnp.concatenate([turned, tail], axis=0).astype(BF)
        for j in range(1, 4):
            cross_x(j).start()

    def spread_context():
        for j in range(1, 4):
            cross_x(j).wait_recv()

        for c in range(8):
            sel[c] = ctx4[captions[c] // 8]
        own_ctx.start()

        def one(i, carry):
            send_ctx(i).start()
            return carry

        lax.fori_loop(1, 16, one, 0)

    def share_context():
        own_ctx.wait()
        share(0).start()

        def one(i, carry):
            send_ctx(i).wait_recv()
            share(i).start()
            return carry

        lax.fori_loop(1, 16, one, 0)

        def got(i, carry):
            share(i).wait()
            return carry

        lax.fori_loop(0, 16, got, 0)

    def at_step(step, when, work):
        @pl.when(step == when)
        def _():
            work()

    locals_of = {
        "middle": again.middle,
        "last": again.last,
        "context": make_context,
        "spread": spread_context,
    }

    def send_win(j):
        to = 4 * clip + (quarter + j) % 4
        return remote(outw.at[j], win.at[quarter], q_send.at[j], q_recv.at[j], to)

    own_win = pltpu.make_async_copy(outw.at[0], win.at[quarter], q_send.at[0])

    def attend(step, carry):
        j = (step // 2 + 1) % 4
        at = 4 * ((quarter + j) % 4)
        for u in range(2):
            h = 2 * (step % 2) + u
            q_rows = heads[0, h, pl.ds(at, 4)].reshape(512, LANE)
            key_rows = heads[1, h].reshape(VT, LANE)
            value_rows = heads[2, h].reshape(VT, LANE)
            score = lax.dot_general(
                q_rows, key_rows, (((1,), (1,)), ((), ())), preferred_element_type=F32
            )
            weight = jnp.exp2(score - jnp.max(score, axis=-1, keepdims=True)).astype(BF)
            value = jnp.dot(weight, value_rows, preferred_element_type=F32)
            value = value / value[:, E : E + 1]
            mix[h] = value.astype(BF)

        @pl.when(step % 2 == 1)
        def _():
            flat = jnp.concatenate([mix[h] for h in range(4)], axis=1)
            outw[j] = lax.dot_general(
                flat, select[quarter], (((1,), (1,)), ((), ())), preferred_element_type=F32
            ).astype(BF)

        @pl.when((step % 2 == 1) & (j > 0))
        def _():
            send_win(j).start()

        for when, work in ATTEND_STEPS:
            at_step(step, when, locals_of[work])
        return carry

    heads_load.wait()
    lax.fori_loop(0, 8, attend, 0)
    own_win.start()

    caption = captions[0]
    for c in range(1, 8):
        caption = jnp.where(clip == c, captions[c], caption)
    pack = caption // 8
    item = caption % 8
    begin = jnp.int32(0)
    finish = jnp.int32(0)
    for n in range(8):
        size = lengths[pack, n]
        begin = begin + jnp.where(n < item, size, 0)
        finish = finish + jnp.where(n <= item, size, 0)
    for copy in loads:
        copy.wait()
    own_win.wait()
    for j in range(1, 4):
        send_win(j).wait()

    def before(n, carry):
        at = pl.multiple_of(256 * n, 256)
        for c in range(3):
            cols = slice(c * WIN, (c + 1) * WIN)
            update = jnp.dot(
                win[0, pl.ds(at, 256)], wob[c, 0:WIN], preferred_element_type=F32
            )
            for i in range(1, 4):
                update = update + jnp.dot(
                    win[i, pl.ds(at, 256)],
                    wob[c, 256 * i : 256 * i + WIN],
                    preferred_element_type=F32,
                )
            first_rows = residual[pl.ds(4 * n, 4), :, cols].reshape(256, WIN)
            hidden[pl.ds(at, 256), cols] = (
                first_rows.astype(F32) + gate[:, cols] * update
            ).astype(BF)
        for c in range(3):
            value = jnp.dot(
                hidden[pl.ds(at, 256)], wcqb[c], preferred_element_type=F32
            )
            query[pl.ds(4 * n, 4), :, c * WIN : (c + 1) * WIN] = (
                (value * QSCALE).astype(BF).reshape(4, 64, WIN)
            )
        for i in range(4):
            cross[i, pl.ds(at, 256)] = jnp.dot(
                query[pl.ds(4 * n, 4), :, 256 * i : 256 * i + WIN].reshape(256, WIN),
                select[i],
                preferred_element_type=F32,
            ).astype(BF)
        return carry

    lax.fori_loop(0, 2, before, 0)
    share_context()

    def send(b):
        return remote(done.at[b], out.at[clip], o_send.at[b], o_recv.at[clip], 8 * quarter + b)

    def send_own(b):
        return pltpu.make_async_copy(done.at[b], out.at[clip], o_send.at[b])

    key_at = lax.broadcasted_iota(jnp.int32, (256, KEYS), 1)
    keep = (key_at >= begin) & (key_at < finish)

    def after(n, carry):
        at = pl.multiple_of(256 * n, 256)

        def four(i, carry):
            for h in range(4):
                at_head = 2 * i + h // 2
                lanes = slice(h * LANE, (h + 1) * LANE)
                score = jnp.dot(
                    cross[i, pl.ds(at, 256), lanes],
                    kv[at_head, h % 2],
                    preferred_element_type=F32,
                )
                score = jnp.where(keep, score, -1e30)
                weight = jnp.exp2(score - jnp.max(score, axis=-1, keepdims=True)).astype(BF)
                value = lax.dot_general(
                    weight,
                    kv[8 + at_head, h % 2],
                    (((1,), (1,)), ((), ())),
                    preferred_element_type=F32,
                )
                value = value / value[:, E : E + 1]
                cross[i, pl.ds(at, 256), lanes] = value.astype(BF)
            return carry

        lax.fori_loop(0, 4, four, 0)
        total = hidden[pl.ds(at, 256)].astype(F32)
        for i in range(4):
            window = lax.dot_general(
                cross[i, pl.ds(at, 256)],
                select[i],
                (((1,), (1,)), ((), ())),
                preferred_element_type=F32,
            ).astype(BF)
            total = total + jnp.dot(
                window, wcob[256 * i : 256 * i + WIN], preferred_element_type=F32
            )
        done[pl.ds(4 * n, 4)] = total.astype(BF).reshape(4, 64, D)
        for i in range(4):
            b = 4 * n + i

            @pl.when(8 * quarter + b == seq)
            def _():
                send_own(b).start()

            @pl.when(8 * quarter + b != seq)
            def _():
                send(b).start()

        return carry

    lax.fori_loop(0, 2, after, 0)

    for j in range(1, 4):
        cross_x(j).wait_send()

    def drain(i, carry):
        send_ctx(i).wait_send()
        return carry

    lax.fori_loop(1, 16, drain, 0)

    def drain_out(b, carry):
        @pl.when(8 * quarter + b == seq)
        def _():
            send_own(b).wait()

        @pl.when(8 * quarter + b != seq)
        def _():
            send(b).wait_send()

        @pl.when(4 * b + z != seq)
        def _():
            remote(done.at[0], out.at[b], o_send.at[0], o_recv.at[b], 4 * b + z).wait_recv()

        return carry

    lax.fori_loop(0, 8, drain_out, 0)


def params(number):
    return pltpu.CompilerParams(
        collective_id=number, has_side_effects=True, vmem_limit_bytes=58 * MIB
    )


def per_device(
    captions,
    lengths,
    clip_order,
    t5_gain,
    w_tq,
    w_tk,
    w_tv,
    w_to,
    w_kv,
    video,
    modulation,
    w_qkv,
    w_o,
    w_cq,
    w_co,
):
    vmem = pl.BlockSpec(memory_space=pltpu.VMEM)
    smem = pl.BlockSpec(memory_space=pltpu.SMEM)
    anywhere = pl.BlockSpec(memory_space=pl.ANY)
    dma = pltpu.SemaphoreType.DMA
    mods = jnp.transpose(modulation, (1, 0, 2))
    heads, quarter_rows, encoded = pl.pallas_call(
        front_kernel,
        out_shape=(
            jax.ShapeDtypeStruct((3, 4, 16, 128, LANE), BF),
            jax.ShapeDtypeStruct((8, 64, D), BF),
            jax.ShapeDtypeStruct((16, DT), BF),
        ),
        in_specs=[smem, vmem, vmem, vmem] + [anywhere] * 6,
        out_specs=(anywhere, anywhere, vmem),
        scratch_shapes=[
            pltpu.VMEM((3, 4, 16, 128, LANE), BF),
            pltpu.VMEM((4, 4, 2, 16, DT), BF),
            pltpu.VMEM((DT, 384), BF),
            pltpu.VMEM((128, DT), BF),
            pltpu.VMEM((3, D, WIN), BF),
            pltpu.VMEM((D, 3 * HP), BF),
            pltpu.VMEM((32, 64, D), BF),
            pltpu.VMEM((KEYS, 384), F32),
            pltpu.VMEM((4, 4, 2, 16, LANE), BF),
            pltpu.VMEM((4, 4, 16, DT), BF),
            pltpu.VMEM((4, 4, 16, DT), BF),
            pltpu.VMEM((4, 4, 16, DT), F32),
            pltpu.VMEM((4, 4, 16, DT), BF),
            pltpu.VMEM((2, 3, 4, 16, HALF), BF),
            pltpu.VMEM((2, 4, 16, HALF), F32),
            pltpu.VMEM((2, 4, 16, HALF), BF),
            pltpu.VMEM((2, 3, 16, HALF), BF),
            dma((8,)),
            dma((20,)),
            dma((20,)),
            dma((16,)),
            dma((16,)),
            dma((16,)),
            dma((16,)),
            dma((13,)),
            dma((13,)),
            dma,
            dma((16,)),
        ],
        compiler_params=params(0),
        name="front",
    )(
        lengths,
        t5_gain.reshape(1, DT),
        captions,
        mods,
        video,
        w_tq,
        w_tk,
        w_tv,
        w_to,
        w_qkv,
    )
    counts = (9, 20, 20, 3, 3, 16, 16, 16, 16, 4, 4, 8, 8)
    return pl.pallas_call(
        attend_kernel,
        out_shape=jax.ShapeDtypeStruct((8, 64, D), BF),
        in_specs=[smem, smem, vmem, vmem, vmem] + [anywhere] * 5,
        out_specs=anywhere,
        scratch_shapes=[
            pltpu.VMEM((3, 4, 16, 128, LANE), BF),
            pltpu.VMEM((4, 4, 2, 16, DT), BF),
            pltpu.VMEM((4, 512, LANE), BF),
            pltpu.VMEM((4, 512, WIN), BF),
            pltpu.VMEM((4, 512, WIN), BF),
            pltpu.VMEM((4, EP, KEYS), BF),
            pltpu.VMEM((8, EP, KEYS), BF),
            pltpu.VMEM((16, 2, LANE, KEYS), BF),
            pltpu.VMEM((4, WIN, HP), BF),
            pltpu.VMEM((8, 64, D), BF),
            pltpu.VMEM((8, 64, D), BF),
            pltpu.VMEM((4, 512, HP), BF),
            pltpu.VMEM((512, D), BF),
            pltpu.VMEM((8, 64, D), BF),
            pltpu.VMEM((3, D, WIN), BF),
            pltpu.VMEM((3, D, WIN), BF),
            pltpu.VMEM((D, D), BF),
        ]
        + [dma((n,)) if n else dma for n in counts],
        compiler_params=params(1),
        name="attend",
    )(
        lengths,
        clip_order,
        encoded,
        mods,
        w_kv.T,
        heads,
        quarter_rows,
        w_o,
        w_cq,
        w_co,
    )


def solution(mesh):
    in_specs = (
        P(("grp", "seq"), None),
        P(),
        P(),
        P(),
        P(None, "seq"),
        P(None, "seq"),
        P(None, "seq"),
        P("seq", None),
        P(None, "seq"),
        P("grp", "seq", None),
        P("grp", None, None),
        P(),
        P(),
        P(),
        P(),
    )
    out_specs = P("grp", "seq", None)
    return jax.shard_map(
        per_device, mesh=mesh, in_specs=in_specs, out_specs=out_specs, check_vma=False
    )
```

```python
import math

import jax
import jax.numpy as jnp
from jax import lax
from jax.experimental import pallas as pl
from jax.experimental.pallas import tpu as pltpu
from jax.sharding import PartitionSpec as P

ET = 64
D = 1152
H = 16
E = 72
DT = 4096
HALF = DT // 2
LANE = 128
WIN = 384
HP = 4 * LANE
KEYS = 512
EP = 80
VT = 2048
MIB = 1024 * 1024
LOG2E = math.log2(math.e)
QSCALE = E ** (-0.5) * LOG2E
BF = jnp.bfloat16
F32 = jnp.float32
ATTEND_STEPS = ((0, "middle"), (3, "last"), (4, "context"), (5, "spread"))
MESH = pl.DeviceIdType.MESH


def place():
    seq = lax.axis_index("seq")
    core = seq % 2
    chip = seq // 2
    return seq, core, chip, chip % 4, chip // 4


def remote(src, dst, send, recv, peer, axis="seq"):
    return pltpu.make_async_remote_copy(
        src_ref=src,
        dst_ref=dst,
        send_sem=send,
        recv_sem=recv,
        device_id={axis: peer},
        device_id_type=MESH,
    )


def greet(peer, axis="seq"):
    pl.semaphore_signal(
        pltpu.get_barrier_semaphore(), inc=1, device_id={axis: peer}, device_id_type=MESH
    )


def head_select(offset):
    row = lax.broadcasted_iota(jnp.int32, (WIN, HP), 0)
    col = lax.broadcasted_iota(jnp.int32, (WIN, HP), 1)
    head = col >> 7
    lane = col & 127
    hit = (row == offset + head * E + lane) & (lane < E)
    return jnp.where(hit, 1.0, 0.0).astype(BF)


class Gather:
    def __init__(self, buf, send, recv):
        seq, core, chip, y, z = place()
        sib = seq + 1 - 2 * core
        first = buf.at[z, y, core, :, pl.ds(0, HALF)]
        second = buf.at[z, y, core, :, pl.ds(HALF, HALF)]
        row = buf.at[z, :, core, :, pl.ds(0, HALF)]
        col = buf.at[:, y, core, :, pl.ds(HALF, HALF)]
        self.a, self.b = [], []
        self.c = [
            remote(row, row, send.at[12], recv.at[12], sib),
            remote(col, col, send.at[13], recv.at[13], sib),
        ]
        for j in range(1, 4):
            py = 8 * z + 2 * ((y + j) % 4) + core
            pz = 8 * ((z + j) % 4) + 2 * y + core
            n = j - 1
            self.a.append(remote(first, first, send.at[n], recv.at[n], py))
            self.a.append(remote(second, second, send.at[n + 3], recv.at[n + 3], pz))
            self.b.append(remote(row, row, send.at[n + 6], recv.at[n + 6], pz))
            self.b.append(remote(col, col, send.at[n + 9], recv.at[n + 9], py))
            near = buf.at[(z + 4 - j) % 4, :, core, :, pl.ds(0, HALF)]
            side = buf.at[:, (y + 4 - j) % 4, core, :, pl.ds(HALF, HALF)]
            self.c.append(remote(near, near, send.at[13 + j], recv.at[13 + j], sib))
            self.c.append(remote(side, side, send.at[16 + j], recv.at[16 + j], sib))

    def start(self):
        for copy in self.a:
            copy.start()

    def middle(self):
        for copy in self.a:
            copy.wait_recv()
        for copy in self.b:
            copy.start()
        for copy in self.c[:2]:
            copy.start()

    def last(self):
        for copy, onward in zip(self.b, self.c[2:]):
            copy.wait_recv()
            onward.start()

    def finish(self):
        for copy in self.c:
            copy.wait_recv()
        for copy in self.a + self.b + self.c:
            copy.wait_send()


def front_kernel(
    lengths,
    gain,
    cap_in,
    mod,
    video,
    wq,
    wk,
    wv,
    wto_in,
    wqkv,
    heads_out,
    quarter_out,
    enc_out,
    heads,
    cap,
    wt,
    wto,
    wwin,
    wpad,
    vid,
    tacc,
    mixb,
    s1,
    r1,
    acc,
    s2,
    r2,
    part,
    s3,
    r3,
    w_sem,
    ag_send,
    ag_recv,
    v_send,
    v_recv,
    f_send,
    f_recv,
    r_send,
    r_recv,
    o_sem,
    k_sem,
):
    seq, core, chip, y, z = place()
    grp = lax.axis_index("grp")
    sib = seq + 1 - 2 * core
    quarter = seq % 4
    clip = seq // 4
    barrier = pltpu.get_barrier_semaphore()
    greet(sib)

    def greet_one(i, carry):
        greet(2 * ((chip + i) % 16) + core)
        return carry

    lax.fori_loop(1, 16, greet_one, 0)

    loads = [
        pltpu.make_async_copy(wq, wt.at[:, pl.ds(0, 128)], w_sem.at[0]),
        pltpu.make_async_copy(wk, wt.at[:, pl.ds(128, 128)], w_sem.at[1]),
        pltpu.make_async_copy(wv, wt.at[:, pl.ds(256, 128)], w_sem.at[2]),
        pltpu.make_async_copy(wto_in, wto, w_sem.at[3]),
    ]
    base = pl.multiple_of(256 * quarter, 128)
    for n in range(3):
        loads.append(
            pltpu.make_async_copy(
                wqkv.at[:, pl.ds(n * D + base, WIN)], wwin.at[n], w_sem.at[4 + n]
            )
        )
    own_video = pltpu.make_async_copy(video.at[clip], vid.at[seq], w_sem.at[7])
    for copy in loads:
        copy.start()
    own_video.start()

    rows = cap_in[...].astype(F32)
    power = jnp.mean(rows * rows, axis=-1, keepdims=True)
    cap[z, y, core] = (rows * lax.rsqrt(power + 1e-06) * gain[...]).astype(BF)

    pl.semaphore_wait(barrier, 16)
    gather = Gather(cap, ag_send, ag_recv)
    gather.start()

    for copy in loads[4:]:
        copy.wait()
    select = head_select(32 * quarter)
    for n in range(3):
        wpad[:, n * HP : (n + 1) * HP] = jnp.dot(
            wwin[n], select, preferred_element_type=F32
        ).astype(BF)
    gather.middle()

    def send_video(i):
        to = (chip + i) % 16
        return remote(video.at[to // 2], vid.at[seq], v_send.at[i], v_recv.at[i], 2 * to + core)

    def start_video(i, carry):
        send_video(i).start()
        return carry

    lax.fori_loop(1, 16, start_video, 0)
    for copy in loads[:4]:
        copy.wait()
    own_video.wait()
    gather.last()

    row_pos = lax.broadcasted_iota(jnp.int32, (KEYS, KEYS), 0)
    col_pos = lax.broadcasted_iota(jnp.int32, (KEYS, KEYS), 1)
    row_seg = jnp.zeros((KEYS, KEYS), jnp.int32)
    col_seg = jnp.zeros((KEYS, KEYS), jnp.int32)
    end = jnp.int32(0)
    for n in range(8):
        end = end + lengths[grp, n]
        row_seg = row_seg + (row_pos >= end).astype(jnp.int32)
        col_seg = col_seg + (col_pos >= end).astype(jnp.int32)
    same = row_seg == col_seg

    gather.finish()
    tacc[...] = jnp.zeros_like(tacc)

    def project(n, carry):
        at = pl.multiple_of(n * 512, 512)
        left = cap[:, :, :, :, pl.ds(at, 512)].reshape(KEYS, 512)
        tacc[...] += jnp.dot(left, wt[pl.ds(at, 512), :], preferred_element_type=F32)
        return carry

    lax.fori_loop(0, 8, project, 0)
    tquery = tacc[:, 0:128].astype(BF)
    tkey = tacc[:, 128:256].astype(BF)
    tvalue = tacc[:, 256:384].astype(BF)
    lane = lax.broadcasted_iota(jnp.int32, (KEYS, LANE), 1)
    mixes = []
    for n in range(2):
        own = (lane >= n * ET) & (lane < (n + 1) * ET)
        head_query = jnp.where(own, tquery.astype(F32), 0.0).astype(BF)
        score = lax.dot_general(
            head_query, tkey, (((1,), (1,)), ((), ())), preferred_element_type=F32
        )
        score = jnp.where(same, score, -1e30)
        weight = jnp.exp(score - jnp.max(score, axis=-1, keepdims=True))
        total = jnp.sum(weight, axis=-1, keepdims=True)
        mixes.append(jnp.dot(weight.astype(BF), tvalue, preferred_element_type=F32) / total)
    mixed = jnp.where(lane < ET, mixes[0], mixes[1]).astype(BF)
    mixb[...] = mixed.reshape(4, 4, 2, 16, LANE)

    def partial_rows(which, out):
        left = mixb[:, :, which].reshape(256, LANE)

        def one(n, carry):
            at = pl.multiple_of(n * 512, 512)
            value = jnp.dot(left, wto[:, pl.ds(at, 512)], preferred_element_type=F32)
            out[:, :, :, pl.ds(at, 512)] = value.reshape(4, 4, 16, 512).astype(out.dtype)
            return carry

        lax.fori_loop(0, 8, one, 0)

    partial_rows(1 - core, s1)
    pair = remote(s1, r1, r_send.at[0], r_recv.at[0], sib)
    pair.start()
    partial_rows(core, acc)
    pair.wait_recv()

    def add_pair(n, carry):
        at = pl.multiple_of(n * 512, 512)
        value = acc[:, :, :, pl.ds(at, 512)] + r1[:, :, :, pl.ds(at, 512)].astype(F32)
        acc[:, :, :, pl.ds(at, 512)] = value
        s2[:, :, :, pl.ds(at, 512)] = value.astype(BF)
        return carry

    lax.fori_loop(0, 8, add_pair, 0)
    second = []
    for j in range(1, 4):
        ty = (y + j) % 4
        tz = (z + j) % 4
        second.append(
            remote(
                s2.at[:, ty, :, pl.ds(0, HALF)],
                r2.at[0, j - 1],
                r_send.at[j],
                r_recv.at[j],
                8 * z + 2 * ty + core,
            )
        )
        second.append(
            remote(
                s2.at[tz, :, :, pl.ds(HALF, HALF)],
                r2.at[1, j - 1],
                r_send.at[3 + j],
                r_recv.at[3 + j],
                8 * tz + 2 * y + core,
            )
        )
    for copy in second:
        copy.start()

    shift = mod[0, pl.ds(clip, 1), :]
    scale = 1.0 + mod[1, pl.ds(clip, 1), :]
    vlane = lax.broadcasted_iota(jnp.int32, (256, HP), 1) & 127

    def forward(i):
        slot = 2 * ((chip + 16 - i) % 16) + core
        return remote(vid.at[slot], vid.at[slot], f_send.at[i], f_recv.at[i], sib)

    def arrive(i):
        send_video(i).wait_recv()
        forward(i).start()

    def norm(at):
        values = vid[pl.ds(2 * at, 2)].reshape(128, D).astype(F32)
        center = values - jnp.mean(values, axis=-1, keepdims=True)
        spread = jnp.mean(center * center, axis=-1, keepdims=True)
        return (center * lax.rsqrt(spread + 1e-06) * scale + shift).astype(BF)

    forward(0).start()
    arrive(1)

    def keep_heads(i):
        at = (chip + 16 - i) % 16
        return pltpu.make_async_copy(heads.at[:, :, at], heads_out.at[:, :, at], k_sem.at[i])

    def project_video(n, carry):
        @pl.when(n < 7)
        def _():
            arrive(2 * n + 2)
            arrive(2 * n + 3)

        forward(2 * n).wait_recv()
        forward(2 * n + 1).wait_recv()
        at0 = (chip + 16 - 2 * n) % 16
        at1 = (chip + 15 - 2 * n) % 16
        normed = jnp.concatenate([norm(at0), norm(at1)], axis=0)
        for which in range(3):
            value = jnp.dot(
                normed, wpad[:, which * HP : (which + 1) * HP], preferred_element_type=F32
            )
            if which == 0:
                value = value * QSCALE
            if which == 2:
                value = jnp.where(vlane == E, 1.0, value)
            value = value.astype(BF)
            for h in range(4):
                piece = value[:, h * LANE : (h + 1) * LANE]
                heads[which, h, at0] = piece[:128]
                heads[which, h, at1] = piece[128:]
        keep_heads(2 * n).start()
        keep_heads(2 * n + 1).start()
        return carry

    lax.fori_loop(0, 8, project_video, 0)
    keep = pltpu.make_async_copy(vid.at[pl.ds(8 * quarter, 8)], quarter_out, o_sem)
    keep.start()

    for copy in second:
        copy.wait_recv()
    for n in range(4):
        first = acc[n, y, :, 0:HALF]
        other = acc[z, n, :, HALF:DT]
        for j in range(3):
            first = first + r2[0, j, n].astype(F32)
            other = other + r2[1, j, n].astype(F32)
        part[0, n] = first
        part[1, n] = other
        s3[0, n] = first.astype(BF)
        s3[1, n] = other.astype(BF)
    third = []
    for j in range(1, 4):
        ty = (y + j) % 4
        tz = (z + j) % 4
        third.append(
            remote(
                s3.at[0, tz],
                r3.at[0, j - 1],
                r_send.at[6 + j],
                r_recv.at[6 + j],
                8 * tz + 2 * y + core,
            )
        )
        third.append(
            remote(
                s3.at[1, ty],
                r3.at[1, j - 1],
                r_send.at[9 + j],
                r_recv.at[9 + j],
                8 * z + 2 * ty + core,
            )
        )
    for copy in third:
        copy.start()
    for copy in third:
        copy.wait_recv()
    first = part[0, z]
    other = part[1, y]
    for j in range(3):
        first = first + r3[0, j].astype(F32)
        other = other + r3[1, j].astype(F32)
    enc_out[:, 0:HALF] = (cap_in[:, 0:HALF].astype(F32) + first).astype(BF)
    enc_out[:, HALF:DT] = (cap_in[:, HALF:DT].astype(F32) + other).astype(BF)

    keep.wait()
    pair.wait_send()
    for copy in second + third:
        copy.wait_send()

    def drain(i, carry):
        send_video(i).wait_send()
        forward(i).wait_send()
        return carry

    lax.fori_loop(1, 16, drain, 0)
    forward(0).wait_send()

    def drain_heads(i, carry):
        keep_heads(i).wait()
        return carry

    lax.fori_loop(0, 16, drain_heads, 0)


def attend_kernel(
    lengths,
    clip_order,
    enc_in,
    mod,
    wkv,
    heads_in,
    residual_in,
    wo,
    wcq,
    wco,
    out,
    heads,
    enc,
    mix,
    outw,
    win,
    ctx4,
    sel,
    kv,
    select,
    query,
    done,
    cross,
    hidden,
    residual,
    wob,
    wcqb,
    wcob,
    w_sem,
    h_send,
    h_recv,
    x_send,
    x_recv,
    c_send,
    c_recv,
    p_send,
    p_recv,
    q_send,
    q_recv,
    o_send,
    o_recv,
):
    seq, core, chip, y, z = place()
    grp = lax.axis_index("grp")
    sib = seq + 1 - 2 * core
    quarter = seq % 4
    clip = seq // 4
    barrier = pltpu.get_barrier_semaphore()

    heads_load = pltpu.make_async_copy(heads_in, heads, w_sem.at[8])
    heads_load.start()

    def greet_one(i, carry):
        greet((seq + i) % 32)
        return carry

    lax.fori_loop(1, 32, greet_one, 0)
    for j in range(1, 4):
        greet((grp + j) % 4, "grp")
    enc[z, y, core] = enc_in[...]
    kv[:, :, EP:LANE, :] = jnp.zeros((16, 2, LANE - EP, KEYS), BF)
    captions = [jnp.int32(0)] * 8
    for i in range(32):
        which = clip_order[i] - grp * 8
        captions = [jnp.where(which == c, i, found) for c, found in enumerate(captions)]
    pl.semaphore_wait(barrier, 34)
    again = Gather(enc, h_send, h_recv)
    again.start()
    loads = [
        pltpu.make_async_copy(wo.at[:, pl.ds(n * WIN, WIN)], wob.at[n], w_sem.at[n])
        for n in range(3)
    ]
    for n in range(3):
        loads.append(
            pltpu.make_async_copy(wcq.at[:, pl.ds(n * WIN, WIN)], wcqb.at[n], w_sem.at[3 + n])
        )
    loads.append(pltpu.make_async_copy(wco, wcob, w_sem.at[6]))
    loads.append(pltpu.make_async_copy(residual_in, residual, w_sem.at[7]))
    for copy in loads:
        copy.start()
    for n in range(4):
        select[n] = head_select(32 * n)
    gate = mod[2, pl.ds(clip, 1), :]

    def cross_x(j):
        mine = ctx4.at[grp]
        return remote(mine, mine, x_send.at[j - 1], x_recv.at[j - 1], (grp + j) % 4, "grp")

    def send_ctx(i):
        to = (chip + i) % 16
        return remote(
            sel.at[to // 2],
            kv.at[chip, core, pl.ds(0, EP)],
            c_send.at[i],
            c_recv.at[i],
            2 * to + core,
        )

    own_ctx = pltpu.make_async_copy(sel.at[clip], kv.at[chip, core, pl.ds(0, EP)], c_send.at[0])

    def share(i):
        rows = kv.at[(chip + 16 - i) % 16, core, pl.ds(0, EP)]
        return remote(rows, rows, p_send.at[i], p_recv.at[i], sib)

    def make_context():
        again.finish()

        def one(n, total):
            at = pl.multiple_of(n * 512, 512)
            left = enc[:, :, :, :, pl.ds(at, 512)].reshape(KEYS, 512)
            return total + lax.dot_general(
                wkv[:, pl.ds(at, 512)],
                left,
                (((1,), (1,)), ((), ())),
                preferred_element_type=F32,
            )

        turned = lax.fori_loop(0, 8, one, jnp.zeros((E, KEYS), F32))
        tail = lax.broadcasted_iota(jnp.int32, (EP - E, KEYS), 0)
        tail = jnp.where(tail == 0, 1.0, 0.0)
        ctx4[grp] = jnp.concatenate([turned, tail], axis=0).astype(BF)
        for j in range(1, 4):
            cross_x(j).start()

    def spread_context():
        for j in range(1, 4):
            cross_x(j).wait_recv()

        for c in range(8):
            sel[c] = ctx4[captions[c] // 8]
        own_ctx.start()

        def one(i, carry):
            send_ctx(i).start()
            return carry

        lax.fori_loop(1, 16, one, 0)

    def share_context():
        own_ctx.wait()
        share(0).start()

        def one(i, carry):
            send_ctx(i).wait_recv()
            share(i).start()
            return carry

        lax.fori_loop(1, 16, one, 0)

        def got(i, carry):
            share(i).wait()
            return carry

        lax.fori_loop(0, 16, got, 0)

    def at_step(step, when, work):
        @pl.when(step == when)
        def _():
            work()

    locals_of = {
        "middle": again.middle,
        "last": again.last,
        "context": make_context,
        "spread": spread_context,
    }

    def send_win(j):
        to = 4 * clip + (quarter + j) % 4
        return remote(outw.at[j], win.at[quarter], q_send.at[j], q_recv.at[j], to)

    own_win = pltpu.make_async_copy(outw.at[0], win.at[quarter], q_send.at[0])

    def attend(step, carry):
        j = (step // 2 + 1) % 4
        at = 4 * ((quarter + j) % 4)
        for u in range(2):
            h = 2 * (step % 2) + u
            q_rows = heads[0, h, pl.ds(at, 4)].reshape(512, LANE)
            key_rows = heads[1, h].reshape(VT, LANE)
            value_rows = heads[2, h].reshape(VT, LANE)
            score = lax.dot_general(
                q_rows, key_rows, (((1,), (1,)), ((), ())), preferred_element_type=F32
            )
            weight = jnp.exp2(score - jnp.max(score, axis=-1, keepdims=True)).astype(BF)
            value = jnp.dot(weight, value_rows, preferred_element_type=F32)
            value = value / value[:, E : E + 1]
            mix[h] = value.astype(BF)

        @pl.when(step % 2 == 1)
        def _():
            flat = jnp.concatenate([mix[h] for h in range(4)], axis=1)
            outw[j] = lax.dot_general(
                flat, select[quarter], (((1,), (1,)), ((), ())), preferred_element_type=F32
            ).astype(BF)

        @pl.when((step % 2 == 1) & (j > 0))
        def _():
            send_win(j).start()

        for when, work in ATTEND_STEPS:
            at_step(step, when, locals_of[work])
        return carry

    heads_load.wait()
    lax.fori_loop(0, 8, attend, 0)
    own_win.start()

    caption = captions[0]
    for c in range(1, 8):
        caption = jnp.where(clip == c, captions[c], caption)
    pack = caption // 8
    item = caption % 8
    begin = jnp.int32(0)
    finish = jnp.int32(0)
    for n in range(8):
        size = lengths[pack, n]
        begin = begin + jnp.where(n < item, size, 0)
        finish = finish + jnp.where(n <= item, size, 0)
    for copy in loads:
        copy.wait()
    own_win.wait()
    for j in range(1, 4):
        send_win(j).wait()

    def before(n, carry):
        at = pl.multiple_of(256 * n, 256)
        for c in range(3):
            cols = slice(c * WIN, (c + 1) * WIN)
            update = jnp.dot(
                win[0, pl.ds(at, 256)], wob[c, 0:WIN], preferred_element_type=F32
            )
            for i in range(1, 4):
                update = update + jnp.dot(
                    win[i, pl.ds(at, 256)],
                    wob[c, 256 * i : 256 * i + WIN],
                    preferred_element_type=F32,
                )
            first_rows = residual[pl.ds(4 * n, 4), :, cols].reshape(256, WIN)
            hidden[pl.ds(at, 256), cols] = (
                first_rows.astype(F32) + gate[:, cols] * update
            ).astype(BF)
        for c in range(3):
            value = jnp.dot(
                hidden[pl.ds(at, 256)], wcqb[c], preferred_element_type=F32
            )
            query[pl.ds(4 * n, 4), :, c * WIN : (c + 1) * WIN] = (
                (value * QSCALE).astype(BF).reshape(4, 64, WIN)
            )
        for i in range(4):
            cross[i, pl.ds(at, 256)] = jnp.dot(
                query[pl.ds(4 * n, 4), :, 256 * i : 256 * i + WIN].reshape(256, WIN),
                select[i],
                preferred_element_type=F32,
            ).astype(BF)
        return carry

    lax.fori_loop(0, 2, before, 0)
    share_context()

    def send(b):
        return remote(done.at[b], out.at[clip], o_send.at[b], o_recv.at[clip], 8 * quarter + b)

    def send_own(b):
        return pltpu.make_async_copy(done.at[b], out.at[clip], o_send.at[b])

    key_at = lax.broadcasted_iota(jnp.int32, (256, KEYS), 1)
    keep = (key_at >= begin) & (key_at < finish)

    def after(n, carry):
        at = pl.multiple_of(256 * n, 256)

        def four(i, carry):
            for h in range(4):
                at_head = 2 * i + h // 2
                lanes = slice(h * LANE, (h + 1) * LANE)
                score = jnp.dot(
                    cross[i, pl.ds(at, 256), lanes],
                    kv[at_head, h % 2],
                    preferred_element_type=F32,
                )
                score = jnp.where(keep, score, -1e30)
                weight = jnp.exp2(score - jnp.max(score, axis=-1, keepdims=True)).astype(BF)
                value = lax.dot_general(
                    weight,
                    kv[8 + at_head, h % 2],
                    (((1,), (1,)), ((), ())),
                    preferred_element_type=F32,
                )
                value = value / value[:, E : E + 1]
                cross[i, pl.ds(at, 256), lanes] = value.astype(BF)
            return carry

        lax.fori_loop(0, 4, four, 0)
        total = hidden[pl.ds(at, 256)].astype(F32)
        for i in range(4):
            window = lax.dot_general(
                cross[i, pl.ds(at, 256)],
                select[i],
                (((1,), (1,)), ((), ())),
                preferred_element_type=F32,
            ).astype(BF)
            total = total + jnp.dot(
                window, wcob[256 * i : 256 * i + WIN], preferred_element_type=F32
            )
        done[pl.ds(4 * n, 4)] = total.astype(BF).reshape(4, 64, D)
        for i in range(4):
            b = 4 * n + i

            @pl.when(8 * quarter + b == seq)
            def _():
                send_own(b).start()

            @pl.when(8 * quarter + b != seq)
            def _():
                send(b).start()

        return carry

    lax.fori_loop(0, 2, after, 0)

    for j in range(1, 4):
        cross_x(j).wait_send()

    def drain(i, carry):
        send_ctx(i).wait_send()
        return carry

    lax.fori_loop(1, 16, drain, 0)

    def drain_out(b, carry):
        @pl.when(8 * quarter + b == seq)
        def _():
            send_own(b).wait()

        @pl.when(8 * quarter + b != seq)
        def _():
            send(b).wait_send()

        @pl.when(4 * b + z != seq)
        def _():
            remote(done.at[0], out.at[b], o_send.at[0], o_recv.at[b], 4 * b + z).wait_recv()

        return carry

    lax.fori_loop(0, 8, drain_out, 0)


def params(number):
    return pltpu.CompilerParams(
        collective_id=number, has_side_effects=True, vmem_limit_bytes=58 * MIB
    )


def per_device(
    captions,
    lengths,
    clip_order,
    t5_gain,
    w_tq,
    w_tk,
    w_tv,
    w_to,
    w_kv,
    video,
    modulation,
    w_qkv,
    w_o,
    w_cq,
    w_co,
):
    vmem = pl.BlockSpec(memory_space=pltpu.VMEM)
    smem = pl.BlockSpec(memory_space=pltpu.SMEM)
    anywhere = pl.BlockSpec(memory_space=pl.ANY)
    dma = pltpu.SemaphoreType.DMA
    mods = jnp.transpose(modulation, (1, 0, 2))
    heads, quarter_rows, encoded = pl.pallas_call(
        front_kernel,
        out_shape=(
            jax.ShapeDtypeStruct((3, 4, 16, 128, LANE), BF),
            jax.ShapeDtypeStruct((8, 64, D), BF),
            jax.ShapeDtypeStruct((16, DT), BF),
        ),
        in_specs=[smem, vmem, vmem, vmem] + [anywhere] * 6,
        out_specs=(anywhere, anywhere, vmem),
        scratch_shapes=[
            pltpu.VMEM((3, 4, 16, 128, LANE), BF),
            pltpu.VMEM((4, 4, 2, 16, DT), BF),
            pltpu.VMEM((DT, 384), BF),
            pltpu.VMEM((128, DT), BF),
            pltpu.VMEM((3, D, WIN), BF),
            pltpu.VMEM((D, 3 * HP), BF),
            pltpu.VMEM((32, 64, D), BF),
            pltpu.VMEM((KEYS, 384), F32),
            pltpu.VMEM((4, 4, 2, 16, LANE), BF),
            pltpu.VMEM((4, 4, 16, DT), BF),
            pltpu.VMEM((4, 4, 16, DT), BF),
            pltpu.VMEM((4, 4, 16, DT), F32),
            pltpu.VMEM((4, 4, 16, DT), BF),
            pltpu.VMEM((2, 3, 4, 16, HALF), BF),
            pltpu.VMEM((2, 4, 16, HALF), F32),
            pltpu.VMEM((2, 4, 16, HALF), BF),
            pltpu.VMEM((2, 3, 16, HALF), BF),
            dma((8,)),
            dma((20,)),
            dma((20,)),
            dma((16,)),
            dma((16,)),
            dma((16,)),
            dma((16,)),
            dma((13,)),
            dma((13,)),
            dma,
            dma((16,)),
        ],
        compiler_params=params(0),
        name="front",
    )(
        lengths,
        t5_gain.reshape(1, DT),
        captions,
        mods,
        video,
        w_tq,
        w_tk,
        w_tv,
        w_to,
        w_qkv,
    )
    counts = (9, 20, 20, 3, 3, 16, 16, 16, 16, 4, 4, 8, 8)
    return pl.pallas_call(
        attend_kernel,
        out_shape=jax.ShapeDtypeStruct((8, 64, D), BF),
        in_specs=[smem, smem, vmem, vmem, vmem] + [anywhere] * 5,
        out_specs=anywhere,
        scratch_shapes=[
            pltpu.VMEM((3, 4, 16, 128, LANE), BF),
            pltpu.VMEM((4, 4, 2, 16, DT), BF),
            pltpu.VMEM((4, 512, LANE), BF),
            pltpu.VMEM((4, 512, WIN), BF),
            pltpu.VMEM((4, 512, WIN), BF),
            pltpu.VMEM((4, EP, KEYS), BF),
            pltpu.VMEM((8, EP, KEYS), BF),
            pltpu.VMEM((16, 2, LANE, KEYS), BF),
            pltpu.VMEM((4, WIN, HP), BF),
            pltpu.VMEM((8, 64, D), BF),
            pltpu.VMEM((8, 64, D), BF),
            pltpu.VMEM((4, 512, HP), BF),
            pltpu.VMEM((512, D), BF),
            pltpu.VMEM((8, 64, D), BF),
            pltpu.VMEM((3, D, WIN), BF),
            pltpu.VMEM((3, D, WIN), BF),
            pltpu.VMEM((D, D), BF),
        ]
        + [dma((n,)) if n else dma for n in counts],
        compiler_params=params(1),
        name="attend",
    )(
        lengths,
        clip_order,
        encoded,
        mods,
        w_kv.T,
        heads,
        quarter_rows,
        w_o,
        w_cq,
        w_co,
    )


def solution(mesh):
    in_specs = (
        P(("grp", "seq"), None),
        P(),
        P(),
        P(),
        P(None, "seq"),
        P(None, "seq"),
        P(None, "seq"),
        P("seq", None),
        P(None, "seq"),
        P("grp", "seq", None),
        P("grp", None, None),
        P(),
        P(),
        P(),
        P(),
    )
    out_specs = P("grp", "seq", None)
    return jax.shard_map(
        per_device, mesh=mesh, in_specs=in_specs, out_specs=out_specs, check_vma=False
    )
```

```python
import math

import jax
import jax.numpy as jnp
from jax import lax
from jax.experimental import pallas as pl
from jax.experimental.pallas import tpu as pltpu
from jax.sharding import PartitionSpec as P

ET = 64
D = 1152
H = 16
E = 72
DT = 4096
HALF = DT // 2
LANE = 128
WIN = 384
HP = 4 * LANE
KEYS = 512
EP = 80
VT = 2048
MIB = 1024 * 1024
LOG2E = math.log2(math.e)
QSCALE = E ** (-0.5) * LOG2E
BF = jnp.bfloat16
F32 = jnp.float32
ATTEND_STEPS = ((0, "middle"), (3, "last"), (4, "context"), (5, "spread"))
MESH = pl.DeviceIdType.MESH


def place():
    seq = lax.axis_index("seq")
    core = seq % 2
    chip = seq // 2
    return seq, core, chip, chip % 4, chip // 4


def remote(src, dst, send, recv, peer, axis="seq"):
    return pltpu.make_async_remote_copy(
        src_ref=src,
        dst_ref=dst,
        send_sem=send,
        recv_sem=recv,
        device_id={axis: peer},
        device_id_type=MESH,
    )


def greet(peer, axis="seq"):
    pl.semaphore_signal(
        pltpu.get_barrier_semaphore(), inc=1, device_id={axis: peer}, device_id_type=MESH
    )


def head_select(offset):
    row = lax.broadcasted_iota(jnp.int32, (WIN, HP), 0)
    col = lax.broadcasted_iota(jnp.int32, (WIN, HP), 1)
    head = col >> 7
    lane = col & 127
    hit = (row == offset + head * E + lane) & (lane < E)
    return jnp.where(hit, 1.0, 0.0).astype(BF)


class Gather:
    def __init__(self, buf, send, recv):
        seq, core, chip, y, z = place()
        sib = seq + 1 - 2 * core
        first = buf.at[z, y, core, :, pl.ds(0, HALF)]
        second = buf.at[z, y, core, :, pl.ds(HALF, HALF)]
        row = buf.at[z, :, core, :, pl.ds(0, HALF)]
        col = buf.at[:, y, core, :, pl.ds(HALF, HALF)]
        self.a, self.b = [], []
        self.c = [
            remote(row, row, send.at[12], recv.at[12], sib),
            remote(col, col, send.at[13], recv.at[13], sib),
        ]
        for j in range(1, 4):
            py = 8 * z + 2 * ((y + j) % 4) + core
            pz = 8 * ((z + j) % 4) + 2 * y + core
            n = j - 1
            self.a.append(remote(first, first, send.at[n], recv.at[n], py))
            self.a.append(remote(second, second, send.at[n + 3], recv.at[n + 3], pz))
            self.b.append(remote(row, row, send.at[n + 6], recv.at[n + 6], pz))
            self.b.append(remote(col, col, send.at[n + 9], recv.at[n + 9], py))
            near = buf.at[(z + 4 - j) % 4, :, core, :, pl.ds(0, HALF)]
            side = buf.at[:, (y + 4 - j) % 4, core, :, pl.ds(HALF, HALF)]
            self.c.append(remote(near, near, send.at[13 + j], recv.at[13 + j], sib))
            self.c.append(remote(side, side, send.at[16 + j], recv.at[16 + j], sib))

    def start(self):
        for copy in self.a:
            copy.start()

    def middle(self):
        for copy in self.a:
            copy.wait_recv()
        for copy in self.b:
            copy.start()
        for copy in self.c[:2]:
            copy.start()

    def last(self):
        for copy, onward in zip(self.b, self.c[2:]):
            copy.wait_recv()
            onward.start()

    def finish(self):
        for copy in self.c:
            copy.wait_recv()
        for copy in self.a + self.b + self.c:
            copy.wait_send()


def front_kernel(
    lengths,
    gain,
    cap_in,
    mod,
    video,
    wq,
    wk,
    wv,
    wto_in,
    wqkv,
    heads_out,
    quarter_out,
    enc_out,
    heads,
    cap,
    wt,
    wto,
    wwin,
    wpad,
    vid,
    tacc,
    mixb,
    s1,
    r1,
    acc,
    s2,
    r2,
    part,
    s3,
    r3,
    w_sem,
    ag_send,
    ag_recv,
    v_send,
    v_recv,
    f_send,
    f_recv,
    r_send,
    r_recv,
    o_sem,
    k_sem,
):
    seq, core, chip, y, z = place()
    grp = lax.axis_index("grp")
    sib = seq + 1 - 2 * core
    quarter = seq % 4
    clip = seq // 4
    barrier = pltpu.get_barrier_semaphore()
    greet(sib)

    def greet_one(i, carry):
        greet(2 * ((chip + i) % 16) + core)
        return carry

    lax.fori_loop(1, 16, greet_one, 0)

    loads = [
        pltpu.make_async_copy(wq, wt.at[:, pl.ds(0, 128)], w_sem.at[0]),
        pltpu.make_async_copy(wk, wt.at[:, pl.ds(128, 128)], w_sem.at[1]),
        pltpu.make_async_copy(wv, wt.at[:, pl.ds(256, 128)], w_sem.at[2]),
        pltpu.make_async_copy(wto_in, wto, w_sem.at[3]),
    ]
    base = pl.multiple_of(256 * quarter, 128)
    for n in range(3):
        loads.append(
            pltpu.make_async_copy(
                wqkv.at[:, pl.ds(n * D + base, WIN)], wwin.at[n], w_sem.at[4 + n]
            )
        )
    own_video = pltpu.make_async_copy(video.at[clip], vid.at[seq], w_sem.at[7])
    for copy in loads:
        copy.start()
    own_video.start()

    rows = cap_in[...].astype(F32)
    power = jnp.mean(rows * rows, axis=-1, keepdims=True)
    cap[z, y, core] = (rows * lax.rsqrt(power + 1e-06) * gain[...]).astype(BF)

    pl.semaphore_wait(barrier, 16)
    gather = Gather(cap, ag_send, ag_recv)
    gather.start()

    def send_video(i):
        to = (chip + i) % 16
        return remote(video.at[to // 2], vid.at[seq], v_send.at[i], v_recv.at[i], 2 * to + core)

    def start_video(i, carry):
        send_video(i).start()
        return carry

    lax.fori_loop(1, 16, start_video, 0)

    for copy in loads[4:]:
        copy.wait()
    select = head_select(32 * quarter)
    for n in range(3):
        wpad[:, n * HP : (n + 1) * HP] = jnp.dot(
            wwin[n], select, preferred_element_type=F32
        ).astype(BF)
    gather.middle()

    for copy in loads[:4]:
        copy.wait()
    own_video.wait()
    gather.last()

    row_pos = lax.broadcasted_iota(jnp.int32, (KEYS, KEYS), 0)
    col_pos = lax.broadcasted_iota(jnp.int32, (KEYS, KEYS), 1)
    row_seg = jnp.zeros((KEYS, KEYS), jnp.int32)
    col_seg = jnp.zeros((KEYS, KEYS), jnp.int32)
    end = jnp.int32(0)
    for n in range(8):
        end = end + lengths[grp, n]
        row_seg = row_seg + (row_pos >= end).astype(jnp.int32)
        col_seg = col_seg + (col_pos >= end).astype(jnp.int32)
    same = row_seg == col_seg

    gather.finish()
    tacc[...] = jnp.zeros_like(tacc)

    def project(n, carry):
        at = pl.multiple_of(n * 512, 512)
        left = cap[:, :, :, :, pl.ds(at, 512)].reshape(KEYS, 512)
        tacc[...] += jnp.dot(left, wt[pl.ds(at, 512), :], preferred_element_type=F32)
        return carry

    lax.fori_loop(0, 8, project, 0)
    tquery = tacc[:, 0:128].astype(BF)
    tkey = tacc[:, 128:256].astype(BF)
    tvalue = tacc[:, 256:384].astype(BF)
    lane = lax.broadcasted_iota(jnp.int32, (KEYS, LANE), 1)
    mixes = []
    for n in range(2):
        own = (lane >= n * ET) & (lane < (n + 1) * ET)
        head_query = jnp.where(own, tquery.astype(F32), 0.0).astype(BF)
        score = lax.dot_general(
            head_query, tkey, (((1,), (1,)), ((), ())), preferred_element_type=F32
        )
        score = jnp.where(same, score, -1e30)
        weight = jnp.exp(score - jnp.max(score, axis=-1, keepdims=True))
        total = jnp.sum(weight, axis=-1, keepdims=True)
        mixes.append(jnp.dot(weight.astype(BF), tvalue, preferred_element_type=F32) / total)
    mixed = jnp.where(lane < ET, mixes[0], mixes[1]).astype(BF)
    mixb[...] = mixed.reshape(4, 4, 2, 16, LANE)

    def partial_rows(which, out):
        left = mixb[:, :, which].reshape(256, LANE)

        def one(n, carry):
            at = pl.multiple_of(n * 512, 512)
            value = jnp.dot(left, wto[:, pl.ds(at, 512)], preferred_element_type=F32)
            out[:, :, :, pl.ds(at, 512)] = value.reshape(4, 4, 16, 512).astype(out.dtype)
            return carry

        lax.fori_loop(0, 8, one, 0)

    partial_rows(1 - core, s1)
    pair = remote(s1, r1, r_send.at[0], r_recv.at[0], sib)
    pair.start()
    partial_rows(core, acc)
    pair.wait_recv()

    def add_pair(n, carry):
        at = pl.multiple_of(n * 512, 512)
        value = acc[:, :, :, pl.ds(at, 512)] + r1[:, :, :, pl.ds(at, 512)].astype(F32)
        acc[:, :, :, pl.ds(at, 512)] = value
        s2[:, :, :, pl.ds(at, 512)] = value.astype(BF)
        return carry

    lax.fori_loop(0, 8, add_pair, 0)
    second = []
    for j in range(1, 4):
        ty = (y + j) % 4
        tz = (z + j) % 4
        second.append(
            remote(
                s2.at[:, ty, :, pl.ds(0, HALF)],
                r2.at[0, j - 1],
                r_send.at[j],
                r_recv.at[j],
                8 * z + 2 * ty + core,
            )
        )
        second.append(
            remote(
                s2.at[tz, :, :, pl.ds(HALF, HALF)],
                r2.at[1, j - 1],
                r_send.at[3 + j],
                r_recv.at[3 + j],
                8 * tz + 2 * y + core,
            )
        )
    for copy in second:
        copy.start()

    shift = mod[0, pl.ds(clip, 1), :]
    scale = 1.0 + mod[1, pl.ds(clip, 1), :]
    vlane = lax.broadcasted_iota(jnp.int32, (256, HP), 1) & 127

    def forward(i):
        slot = 2 * ((chip + 16 - i) % 16) + core
        return remote(vid.at[slot], vid.at[slot], f_send.at[i], f_recv.at[i], sib)

    def arrive(i):
        send_video(i).wait_recv()
        forward(i).start()

    def norm(at):
        values = vid[pl.ds(2 * at, 2)].reshape(128, D).astype(F32)
        center = values - jnp.mean(values, axis=-1, keepdims=True)
        spread = jnp.mean(center * center, axis=-1, keepdims=True)
        return (center * lax.rsqrt(spread + 1e-06) * scale + shift).astype(BF)

    forward(0).start()
    arrive(1)

    def keep_heads(i):
        at = (chip + 16 - i) % 16
        return pltpu.make_async_copy(heads.at[:, :, at], heads_out.at[:, :, at], k_sem.at[i])

    def project_video(n, carry):
        @pl.when(n < 7)
        def _():
            arrive(2 * n + 2)
            arrive(2 * n + 3)

        forward(2 * n).wait_recv()
        forward(2 * n + 1).wait_recv()
        at0 = (chip + 16 - 2 * n) % 16
        at1 = (chip + 15 - 2 * n) % 16
        normed = jnp.concatenate([norm(at0), norm(at1)], axis=0)
        for which in range(3):
            value = jnp.dot(
                normed, wpad[:, which * HP : (which + 1) * HP], preferred_element_type=F32
            )
            if which == 0:
                value = value * QSCALE
            if which == 2:
                value = jnp.where(vlane == E, 1.0, value)
            value = value.astype(BF)
            for h in range(4):
                piece = value[:, h * LANE : (h + 1) * LANE]
                heads[which, h, at0] = piece[:128]
                heads[which, h, at1] = piece[128:]
        keep_heads(2 * n).start()
        keep_heads(2 * n + 1).start()
        return carry

    lax.fori_loop(0, 8, project_video, 0)
    keep = pltpu.make_async_copy(vid.at[pl.ds(8 * quarter, 8)], quarter_out, o_sem)
    keep.start()

    for copy in second:
        copy.wait_recv()
    for n in range(4):
        first = acc[n, y, :, 0:HALF]
        other = acc[z, n, :, HALF:DT]
        for j in range(3):
            first = first + r2[0, j, n].astype(F32)
            other = other + r2[1, j, n].astype(F32)
        part[0, n] = first
        part[1, n] = other
        s3[0, n] = first.astype(BF)
        s3[1, n] = other.astype(BF)
    third = []
    for j in range(1, 4):
        ty = (y + j) % 4
        tz = (z + j) % 4
        third.append(
            remote(
                s3.at[0, tz],
                r3.at[0, j - 1],
                r_send.at[6 + j],
                r_recv.at[6 + j],
                8 * tz + 2 * y + core,
            )
        )
        third.append(
            remote(
                s3.at[1, ty],
                r3.at[1, j - 1],
                r_send.at[9 + j],
                r_recv.at[9 + j],
                8 * z + 2 * ty + core,
            )
        )
    for copy in third:
        copy.start()
    for copy in third:
        copy.wait_recv()
    first = part[0, z]
    other = part[1, y]
    for j in range(3):
        first = first + r3[0, j].astype(F32)
        other = other + r3[1, j].astype(F32)
    enc_out[:, 0:HALF] = (cap_in[:, 0:HALF].astype(F32) + first).astype(BF)
    enc_out[:, HALF:DT] = (cap_in[:, HALF:DT].astype(F32) + other).astype(BF)

    keep.wait()
    pair.wait_send()
    for copy in second + third:
        copy.wait_send()

    def drain(i, carry):
        send_video(i).wait_send()
        forward(i).wait_send()
        return carry

    lax.fori_loop(1, 16, drain, 0)
    forward(0).wait_send()

    def drain_heads(i, carry):
        keep_heads(i).wait()
        return carry

    lax.fori_loop(0, 16, drain_heads, 0)


def attend_kernel(
    lengths,
    clip_order,
    enc_in,
    mod,
    wkv,
    heads_in,
    residual_in,
    wo,
    wcq,
    wco,
    out,
    heads,
    enc,
    mix,
    outw,
    win,
    ctx4,
    sel,
    kv,
    select,
    query,
    done,
    cross,
    hidden,
    residual,
    wob,
    wcqb,
    wcob,
    w_sem,
    h_send,
    h_recv,
    x_send,
    x_recv,
    c_send,
    c_recv,
    p_send,
    p_recv,
    q_send,
    q_recv,
    o_send,
    o_recv,
):
    seq, core, chip, y, z = place()
    grp = lax.axis_index("grp")
    sib = seq + 1 - 2 * core
    quarter = seq % 4
    clip = seq // 4
    barrier = pltpu.get_barrier_semaphore()

    heads_load = pltpu.make_async_copy(heads_in, heads, w_sem.at[8])
    heads_load.start()

    def greet_one(i, carry):
        greet((seq + i) % 32)
        return carry

    lax.fori_loop(1, 32, greet_one, 0)
    for j in range(1, 4):
        greet((grp + j) % 4, "grp")
    enc[z, y, core] = enc_in[...]
    kv[:, :, EP:LANE, :] = jnp.zeros((16, 2, LANE - EP, KEYS), BF)
    captions = [jnp.int32(0)] * 8
    for i in range(32):
        which = clip_order[i] - grp * 8
        captions = [jnp.where(which == c, i, found) for c, found in enumerate(captions)]
    pl.semaphore_wait(barrier, 34)
    again = Gather(enc, h_send, h_recv)
    again.start()
    loads = [
        pltpu.make_async_copy(wo.at[:, pl.ds(n * WIN, WIN)], wob.at[n], w_sem.at[n])
        for n in range(3)
    ]
    for n in range(3):
        loads.append(
            pltpu.make_async_copy(wcq.at[:, pl.ds(n * WIN, WIN)], wcqb.at[n], w_sem.at[3 + n])
        )
    loads.append(pltpu.make_async_copy(wco, wcob, w_sem.at[6]))
    loads.append(pltpu.make_async_copy(residual_in, residual, w_sem.at[7]))
    for copy in loads:
        copy.start()
    for n in range(4):
        select[n] = head_select(32 * n)
    gate = mod[2, pl.ds(clip, 1), :]

    def cross_x(j):
        mine = ctx4.at[grp]
        return remote(mine, mine, x_send.at[j - 1], x_recv.at[j - 1], (grp + j) % 4, "grp")

    def send_ctx(i):
        to = (chip + i) % 16
        return remote(
            sel.at[to // 2],
            kv.at[chip, core, pl.ds(0, EP)],
            c_send.at[i],
            c_recv.at[i],
            2 * to + core,
        )

    own_ctx = pltpu.make_async_copy(sel.at[clip], kv.at[chip, core, pl.ds(0, EP)], c_send.at[0])

    def share(i):
        rows = kv.at[(chip + 16 - i) % 16, core, pl.ds(0, EP)]
        return remote(rows, rows, p_send.at[i], p_recv.at[i], sib)

    def make_context():
        again.finish()

        def one(n, total):
            at = pl.multiple_of(n * 512, 512)
            left = enc[:, :, :, :, pl.ds(at, 512)].reshape(KEYS, 512)
            return total + lax.dot_general(
                wkv[:, pl.ds(at, 512)],
                left,
                (((1,), (1,)), ((), ())),
                preferred_element_type=F32,
            )

        turned = lax.fori_loop(0, 8, one, jnp.zeros((E, KEYS), F32))
        tail = lax.broadcasted_iota(jnp.int32, (EP - E, KEYS), 0)
        tail = jnp.where(tail == 0, 1.0, 0.0)
        ctx4[grp] = jnp.concatenate([turned, tail], axis=0).astype(BF)
        for j in range(1, 4):
            cross_x(j).start()

    def spread_context():
        for j in range(1, 4):
            cross_x(j).wait_recv()

        for c in range(8):
            sel[c] = ctx4[captions[c] // 8]
        own_ctx.start()

        def one(i, carry):
            send_ctx(i).start()
            return carry

        lax.fori_loop(1, 16, one, 0)

    def share_context():
        own_ctx.wait()
        share(0).start()

        def one(i, carry):
            send_ctx(i).wait_recv()
            share(i).start()
            return carry

        lax.fori_loop(1, 16, one, 0)

        def got(i, carry):
            share(i).wait()
            return carry

        lax.fori_loop(0, 16, got, 0)

    def at_step(step, when, work):
        @pl.when(step == when)
        def _():
            work()

    locals_of = {
        "middle": again.middle,
        "last": again.last,
        "context": make_context,
        "spread": spread_context,
    }

    def send_win(j):
        to = 4 * clip + (quarter + j) % 4
        return remote(outw.at[j], win.at[quarter], q_send.at[j], q_recv.at[j], to)

    own_win = pltpu.make_async_copy(outw.at[0], win.at[quarter], q_send.at[0])

    def attend(step, carry):
        j = (step // 2 + 1) % 4
        at = 4 * ((quarter + j) % 4)
        for u in range(2):
            h = 2 * (step % 2) + u
            q_rows = heads[0, h, pl.ds(at, 4)].reshape(512, LANE)
            key_rows = heads[1, h].reshape(VT, LANE)
            value_rows = heads[2, h].reshape(VT, LANE)
            score = lax.dot_general(
                q_rows, key_rows, (((1,), (1,)), ((), ())), preferred_element_type=F32
            )
            weight = jnp.exp2(score - jnp.max(score, axis=-1, keepdims=True)).astype(BF)
            value = jnp.dot(weight, value_rows, preferred_element_type=F32)
            value = value / value[:, E : E + 1]
            mix[h] = value.astype(BF)

        @pl.when(step % 2 == 1)
        def _():
            flat = jnp.concatenate([mix[h] for h in range(4)], axis=1)
            outw[j] = lax.dot_general(
                flat, select[quarter], (((1,), (1,)), ((), ())), preferred_element_type=F32
            ).astype(BF)

        @pl.when((step % 2 == 1) & (j > 0))
        def _():
            send_win(j).start()

        for when, work in ATTEND_STEPS:
            at_step(step, when, locals_of[work])
        return carry

    heads_load.wait()
    lax.fori_loop(0, 8, attend, 0)
    own_win.start()

    caption = captions[0]
    for c in range(1, 8):
        caption = jnp.where(clip == c, captions[c], caption)
    pack = caption // 8
    item = caption % 8
    begin = jnp.int32(0)
    finish = jnp.int32(0)
    for n in range(8):
        size = lengths[pack, n]
        begin = begin + jnp.where(n < item, size, 0)
        finish = finish + jnp.where(n <= item, size, 0)
    for copy in loads:
        copy.wait()
    own_win.wait()
    for j in range(1, 4):
        send_win(j).wait()

    def before(n, carry):
        at = pl.multiple_of(256 * n, 256)
        for c in range(3):
            cols = slice(c * WIN, (c + 1) * WIN)
            update = jnp.dot(
                win[0, pl.ds(at, 256)], wob[c, 0:WIN], preferred_element_type=F32
            )
            for i in range(1, 4):
                update = update + jnp.dot(
                    win[i, pl.ds(at, 256)],
                    wob[c, 256 * i : 256 * i + WIN],
                    preferred_element_type=F32,
                )
            first_rows = residual[pl.ds(4 * n, 4), :, cols].reshape(256, WIN)
            hidden[pl.ds(at, 256), cols] = (
                first_rows.astype(F32) + gate[:, cols] * update
            ).astype(BF)
        for c in range(3):
            value = jnp.dot(
                hidden[pl.ds(at, 256)], wcqb[c], preferred_element_type=F32
            )
            query[pl.ds(4 * n, 4), :, c * WIN : (c + 1) * WIN] = (
                (value * QSCALE).astype(BF).reshape(4, 64, WIN)
            )
        for i in range(4):
            cross[i, pl.ds(at, 256)] = jnp.dot(
                query[pl.ds(4 * n, 4), :, 256 * i : 256 * i + WIN].reshape(256, WIN),
                select[i],
                preferred_element_type=F32,
            ).astype(BF)
        return carry

    lax.fori_loop(0, 2, before, 0)
    share_context()

    def send(b):
        return remote(done.at[b], out.at[clip], o_send.at[b], o_recv.at[clip], 8 * quarter + b)

    def send_own(b):
        return pltpu.make_async_copy(done.at[b], out.at[clip], o_send.at[b])

    key_at = lax.broadcasted_iota(jnp.int32, (256, KEYS), 1)
    keep = (key_at >= begin) & (key_at < finish)

    def after(n, carry):
        at = pl.multiple_of(256 * n, 256)

        def four(i, carry):
            for h in range(4):
                at_head = 2 * i + h // 2
                lanes = slice(h * LANE, (h + 1) * LANE)
                score = jnp.dot(
                    cross[i, pl.ds(at, 256), lanes],
                    kv[at_head, h % 2],
                    preferred_element_type=F32,
                )
                score = jnp.where(keep, score, -1e30)
                weight = jnp.exp2(score - jnp.max(score, axis=-1, keepdims=True)).astype(BF)
                value = lax.dot_general(
                    weight,
                    kv[8 + at_head, h % 2],
                    (((1,), (1,)), ((), ())),
                    preferred_element_type=F32,
                )
                value = value / value[:, E : E + 1]
                cross[i, pl.ds(at, 256), lanes] = value.astype(BF)
            return carry

        lax.fori_loop(0, 4, four, 0)
        total = hidden[pl.ds(at, 256)].astype(F32)
        for i in range(4):
            window = lax.dot_general(
                cross[i, pl.ds(at, 256)],
                select[i],
                (((1,), (1,)), ((), ())),
                preferred_element_type=F32,
            ).astype(BF)
            total = total + jnp.dot(
                window, wcob[256 * i : 256 * i + WIN], preferred_element_type=F32
            )
        done[pl.ds(4 * n, 4)] = total.astype(BF).reshape(4, 64, D)
        for i in range(4):
            b = 4 * n + i

            @pl.when(8 * quarter + b == seq)
            def _():
                send_own(b).start()

            @pl.when(8 * quarter + b != seq)
            def _():
                send(b).start()

        return carry

    lax.fori_loop(0, 2, after, 0)

    for j in range(1, 4):
        cross_x(j).wait_send()

    def drain(i, carry):
        send_ctx(i).wait_send()
        return carry

    lax.fori_loop(1, 16, drain, 0)

    def drain_out(b, carry):
        @pl.when(8 * quarter + b == seq)
        def _():
            send_own(b).wait()

        @pl.when(8 * quarter + b != seq)
        def _():
            send(b).wait_send()

        @pl.when(4 * b + z != seq)
        def _():
            remote(done.at[0], out.at[b], o_send.at[0], o_recv.at[b], 4 * b + z).wait_recv()

        return carry

    lax.fori_loop(0, 8, drain_out, 0)


def params(number):
    return pltpu.CompilerParams(
        collective_id=number, has_side_effects=True, vmem_limit_bytes=58 * MIB
    )


def per_device(
    captions,
    lengths,
    clip_order,
    t5_gain,
    w_tq,
    w_tk,
    w_tv,
    w_to,
    w_kv,
    video,
    modulation,
    w_qkv,
    w_o,
    w_cq,
    w_co,
):
    vmem = pl.BlockSpec(memory_space=pltpu.VMEM)
    smem = pl.BlockSpec(memory_space=pltpu.SMEM)
    anywhere = pl.BlockSpec(memory_space=pl.ANY)
    dma = pltpu.SemaphoreType.DMA
    mods = jnp.transpose(modulation, (1, 0, 2))
    heads, quarter_rows, encoded = pl.pallas_call(
        front_kernel,
        out_shape=(
            jax.ShapeDtypeStruct((3, 4, 16, 128, LANE), BF),
            jax.ShapeDtypeStruct((8, 64, D), BF),
            jax.ShapeDtypeStruct((16, DT), BF),
        ),
        in_specs=[smem, vmem, vmem, vmem] + [anywhere] * 6,
        out_specs=(anywhere, anywhere, vmem),
        scratch_shapes=[
            pltpu.VMEM((3, 4, 16, 128, LANE), BF),
            pltpu.VMEM((4, 4, 2, 16, DT), BF),
            pltpu.VMEM((DT, 384), BF),
            pltpu.VMEM((128, DT), BF),
            pltpu.VMEM((3, D, WIN), BF),
            pltpu.VMEM((D, 3 * HP), BF),
            pltpu.VMEM((32, 64, D), BF),
            pltpu.VMEM((KEYS, 384), F32),
            pltpu.VMEM((4, 4, 2, 16, LANE), BF),
            pltpu.VMEM((4, 4, 16, DT), BF),
            pltpu.VMEM((4, 4, 16, DT), BF),
            pltpu.VMEM((4, 4, 16, DT), F32),
            pltpu.VMEM((4, 4, 16, DT), BF),
            pltpu.VMEM((2, 3, 4, 16, HALF), BF),
            pltpu.VMEM((2, 4, 16, HALF), F32),
            pltpu.VMEM((2, 4, 16, HALF), BF),
            pltpu.VMEM((2, 3, 16, HALF), BF),
            dma((8,)),
            dma((20,)),
            dma((20,)),
            dma((16,)),
            dma((16,)),
            dma((16,)),
            dma((16,)),
            dma((13,)),
            dma((13,)),
            dma,
            dma((16,)),
        ],
        compiler_params=params(0),
        name="front",
    )(
        lengths,
        t5_gain.reshape(1, DT),
        captions,
        mods,
        video,
        w_tq,
        w_tk,
        w_tv,
        w_to,
        w_qkv,
    )
    counts = (9, 20, 20, 3, 3, 16, 16, 16, 16, 4, 4, 8, 8)
    return pl.pallas_call(
        attend_kernel,
        out_shape=jax.ShapeDtypeStruct((8, 64, D), BF),
        in_specs=[smem, smem, vmem, vmem, vmem] + [anywhere] * 5,
        out_specs=anywhere,
        scratch_shapes=[
            pltpu.VMEM((3, 4, 16, 128, LANE), BF),
            pltpu.VMEM((4, 4, 2, 16, DT), BF),
            pltpu.VMEM((4, 512, LANE), BF),
            pltpu.VMEM((4, 512, WIN), BF),
            pltpu.VMEM((4, 512, WIN), BF),
            pltpu.VMEM((4, EP, KEYS), BF),
            pltpu.VMEM((8, EP, KEYS), BF),
            pltpu.VMEM((16, 2, LANE, KEYS), BF),
            pltpu.VMEM((4, WIN, HP), BF),
            pltpu.VMEM((8, 64, D), BF),
            pltpu.VMEM((8, 64, D), BF),
            pltpu.VMEM((4, 512, HP), BF),
            pltpu.VMEM((512, D), BF),
            pltpu.VMEM((8, 64, D), BF),
            pltpu.VMEM((3, D, WIN), BF),
            pltpu.VMEM((3, D, WIN), BF),
            pltpu.VMEM((D, D), BF),
        ]
        + [dma((n,)) if n else dma for n in counts],
        compiler_params=params(1),
        name="attend",
    )(
        lengths,
        clip_order,
        encoded,
        mods,
        w_kv.T,
        heads,
        quarter_rows,
        w_o,
        w_cq,
        w_co,
    )


def solution(mesh):
    in_specs = (
        P(("grp", "seq"), None),
        P(),
        P(),
        P(),
        P(None, "seq"),
        P(None, "seq"),
        P(None, "seq"),
        P("seq", None),
        P(None, "seq"),
        P("grp", "seq", None),
        P("grp", None, None),
        P(),
        P(),
        P(),
        P(),
    )
    out_specs = P("grp", "seq", None)
    return jax.shard_map(
        per_device, mesh=mesh, in_specs=in_specs, out_specs=out_specs, check_vma=False
    )
```

```python
import math

import jax
import jax.numpy as jnp
from jax import lax
from jax.experimental import pallas as pl
from jax.experimental.pallas import tpu as pltpu
from jax.sharding import PartitionSpec as P

ET = 64
D = 1152
H = 16
E = 72
DT = 4096
HALF = DT // 2
LANE = 128
WIN = 384
HP = 4 * LANE
KEYS = 512
EP = 80
VT = 2048
MIB = 1024 * 1024
LOG2E = math.log2(math.e)
QSCALE = E ** (-0.5) * LOG2E
BF = jnp.bfloat16
F32 = jnp.float32
ATTEND_STEPS = ((0, "middle"), (3, "last"), (4, "context"), (5, "spread"))
MESH = pl.DeviceIdType.MESH


def place():
    seq = lax.axis_index("seq")
    core = seq % 2
    chip = seq // 2
    return seq, core, chip, chip % 4, chip // 4


def remote(src, dst, send, recv, peer, axis="seq"):
    return pltpu.make_async_remote_copy(
        src_ref=src,
        dst_ref=dst,
        send_sem=send,
        recv_sem=recv,
        device_id={axis: peer},
        device_id_type=MESH,
    )


def greet(peer, axis="seq"):
    pl.semaphore_signal(
        pltpu.get_barrier_semaphore(), inc=1, device_id={axis: peer}, device_id_type=MESH
    )


def head_select(offset):
    row = lax.broadcasted_iota(jnp.int32, (WIN, HP), 0)
    col = lax.broadcasted_iota(jnp.int32, (WIN, HP), 1)
    head = col >> 7
    lane = col & 127
    hit = (row == offset + head * E + lane) & (lane < E)
    return jnp.where(hit, 1.0, 0.0).astype(BF)


class Gather:
    def __init__(self, buf, send, recv):
        seq, core, chip, y, z = place()
        sib = seq + 1 - 2 * core
        first = buf.at[z, y, core, :, pl.ds(0, HALF)]
        second = buf.at[z, y, core, :, pl.ds(HALF, HALF)]
        row = buf.at[z, :, core, :, pl.ds(0, HALF)]
        col = buf.at[:, y, core, :, pl.ds(HALF, HALF)]
        self.a, self.b = [], []
        self.c = [
            remote(row, row, send.at[12], recv.at[12], sib),
            remote(col, col, send.at[13], recv.at[13], sib),
        ]
        for j in range(1, 4):
            py = 8 * z + 2 * ((y + j) % 4) + core
            pz = 8 * ((z + j) % 4) + 2 * y + core
            n = j - 1
            self.a.append(remote(first, first, send.at[n], recv.at[n], py))
            self.a.append(remote(second, second, send.at[n + 3], recv.at[n + 3], pz))
            self.b.append(remote(row, row, send.at[n + 6], recv.at[n + 6], pz))
            self.b.append(remote(col, col, send.at[n + 9], recv.at[n + 9], py))
            near = buf.at[(z + 4 - j) % 4, :, core, :, pl.ds(0, HALF)]
            side = buf.at[:, (y + 4 - j) % 4, core, :, pl.ds(HALF, HALF)]
            self.c.append(remote(near, near, send.at[13 + j], recv.at[13 + j], sib))
            self.c.append(remote(side, side, send.at[16 + j], recv.at[16 + j], sib))

    def start(self):
        for copy in self.a:
            copy.start()

    def middle(self):
        for copy in self.a:
            copy.wait_recv()
        for copy in self.b:
            copy.start()
        for copy in self.c[:2]:
            copy.start()

    def last(self):
        for copy, onward in zip(self.b, self.c[2:]):
            copy.wait_recv()
            onward.start()

    def finish(self):
        for copy in self.c:
            copy.wait_recv()
        for copy in self.a + self.b + self.c:
            copy.wait_send()


def front_kernel(
    lengths,
    gain,
    cap_in,
    mod,
    video,
    wq,
    wk,
    wv,
    wto_in,
    wqkv,
    heads_out,
    quarter_out,
    enc_out,
    heads,
    cap,
    wt,
    wto,
    wwin,
    wpad,
    vid,
    tacc,
    mixb,
    s1,
    r1,
    acc,
    s2,
    r2,
    part,
    s3,
    r3,
    w_sem,
    ag_send,
    ag_recv,
    v_send,
    v_recv,
    f_send,
    f_recv,
    r_send,
    r_recv,
    o_sem,
    k_sem,
):
    seq, core, chip, y, z = place()
    grp = lax.axis_index("grp")
    sib = seq + 1 - 2 * core
    quarter = seq % 4
    clip = seq // 4
    barrier = pltpu.get_barrier_semaphore()
    greet(sib)

    def greet_one(i, carry):
        greet(2 * ((chip + i) % 16) + core)
        return carry

    lax.fori_loop(1, 16, greet_one, 0)

    loads = [
        pltpu.make_async_copy(wq, wt.at[:, pl.ds(0, 128)], w_sem.at[0]),
        pltpu.make_async_copy(wk, wt.at[:, pl.ds(128, 128)], w_sem.at[1]),
        pltpu.make_async_copy(wv, wt.at[:, pl.ds(256, 128)], w_sem.at[2]),
        pltpu.make_async_copy(wto_in, wto, w_sem.at[3]),
    ]
    base = pl.multiple_of(256 * quarter, 128)
    for n in range(3):
        loads.append(
            pltpu.make_async_copy(
                wqkv.at[:, pl.ds(n * D + base, WIN)], wwin.at[n], w_sem.at[4 + n]
            )
        )
    own_video = pltpu.make_async_copy(video.at[clip], vid.at[seq], w_sem.at[7])
    for copy in loads:
        copy.start()
    own_video.start()

    rows = cap_in[...].astype(F32)
    power = jnp.mean(rows * rows, axis=-1, keepdims=True)
    cap[z, y, core] = (rows * lax.rsqrt(power + 1e-06) * gain[...]).astype(BF)

    pl.semaphore_wait(barrier, 16)
    gather = Gather(cap, ag_send, ag_recv)
    gather.start()

    for copy in loads[4:]:
        copy.wait()
    select = head_select(32 * quarter)
    for n in range(3):
        wpad[:, n * HP : (n + 1) * HP] = jnp.dot(
            wwin[n], select, preferred_element_type=F32
        ).astype(BF)
    gather.middle()

    def send_video(i):
        to = (chip + i) % 16
        return remote(video.at[to // 2], vid.at[seq], v_send.at[i], v_recv.at[i], 2 * to + core)

    def start_video(i, carry):
        send_video(i).start()
        return carry

    lax.fori_loop(1, 16, start_video, 0)
    for copy in loads[:4]:
        copy.wait()
    own_video.wait()
    gather.last()

    row_pos = lax.broadcasted_iota(jnp.int32, (KEYS, KEYS), 0)
    col_pos = lax.broadcasted_iota(jnp.int32, (KEYS, KEYS), 1)
    row_seg = jnp.zeros((KEYS, KEYS), jnp.int32)
    col_seg = jnp.zeros((KEYS, KEYS), jnp.int32)
    end = jnp.int32(0)
    for n in range(8):
        end = end + lengths[grp, n]
        row_seg = row_seg + (row_pos >= end).astype(jnp.int32)
        col_seg = col_seg + (col_pos >= end).astype(jnp.int32)
    same = row_seg == col_seg

    gather.finish()
    tacc[...] = jnp.zeros_like(tacc)

    def project(n, carry):
        at = pl.multiple_of(n * 512, 512)
        left = cap[:, :, :, :, pl.ds(at, 512)].reshape(KEYS, 512)
        tacc[...] += jnp.dot(left, wt[pl.ds(at, 512), :], preferred_element_type=F32)
        return carry

    lax.fori_loop(0, 8, project, 0)
    tquery = tacc[:, 0:128].astype(BF)
    tkey = tacc[:, 128:256].astype(BF)
    tvalue = tacc[:, 256:384].astype(BF)
    lane = lax.broadcasted_iota(jnp.int32, (KEYS, LANE), 1)
    mixes = []
    for n in range(2):
        own = (lane >= n * ET) & (lane < (n + 1) * ET)
        head_query = jnp.where(own, tquery.astype(F32), 0.0).astype(BF)
        score = lax.dot_general(
            head_query, tkey, (((1,), (1,)), ((), ())), preferred_element_type=F32
        )
        score = jnp.where(same, score, -1e30)
        weight = jnp.exp(score - jnp.max(score, axis=-1, keepdims=True))
        total = jnp.sum(weight, axis=-1, keepdims=True)
        mixes.append(jnp.dot(weight.astype(BF), tvalue, preferred_element_type=F32) / total)
    mixed = jnp.where(lane < ET, mixes[0], mixes[1]).astype(BF)
    mixb[...] = mixed.reshape(4, 4, 2, 16, LANE)

    def partial_rows(which, out):
        left = mixb[:, :, which].reshape(256, LANE)

        def one(n, carry):
            at = pl.multiple_of(n * 512, 512)
            value = jnp.dot(left, wto[:, pl.ds(at, 512)], preferred_element_type=F32)
            out[:, :, :, pl.ds(at, 512)] = value.reshape(4, 4, 16, 512).astype(out.dtype)
            return carry

        lax.fori_loop(0, 8, one, 0)

    partial_rows(1 - core, s1)
    pair = remote(s1, r1, r_send.at[0], r_recv.at[0], sib)
    pair.start()
    partial_rows(core, acc)
    pair.wait_recv()

    def add_pair(n, carry):
        at = pl.multiple_of(n * 512, 512)
        value = acc[:, :, :, pl.ds(at, 512)] + r1[:, :, :, pl.ds(at, 512)].astype(F32)
        acc[:, :, :, pl.ds(at, 512)] = value
        s2[:, :, :, pl.ds(at, 512)] = value.astype(BF)
        return carry

    lax.fori_loop(0, 8, add_pair, 0)
    second = []
    for j in range(1, 4):
        ty = (y + j) % 4
        tz = (z + j) % 4
        second.append(
            remote(
                s2.at[:, ty, :, pl.ds(0, HALF)],
                r2.at[0, j - 1],
                r_send.at[j],
                r_recv.at[j],
                8 * z + 2 * ty + core,
            )
        )
        second.append(
            remote(
                s2.at[tz, :, :, pl.ds(HALF, HALF)],
                r2.at[1, j - 1],
                r_send.at[3 + j],
                r_recv.at[3 + j],
                8 * tz + 2 * y + core,
            )
        )
    for copy in second:
        copy.start()

    shift = mod[0, pl.ds(clip, 1), :]
    scale = 1.0 + mod[1, pl.ds(clip, 1), :]
    vlane = lax.broadcasted_iota(jnp.int32, (256, HP), 1) & 127

    def forward(i):
        slot = 2 * ((chip + 16 - i) % 16) + core
        return remote(vid.at[slot], vid.at[slot], f_send.at[i], f_recv.at[i], sib)

    def arrive(i):
        send_video(i).wait_recv()
        forward(i).start()

    def norm(at):
        values = vid[pl.ds(2 * at, 2)].reshape(128, D).astype(F32)
        center = values - jnp.mean(values, axis=-1, keepdims=True)
        spread = jnp.mean(center * center, axis=-1, keepdims=True)
        return (center * lax.rsqrt(spread + 1e-06) * scale + shift).astype(BF)

    forward(0).start()
    arrive(1)

    def keep_heads(i):
        at = (chip + 16 - i) % 16
        return pltpu.make_async_copy(heads.at[:, :, at], heads_out.at[:, :, at], k_sem.at[i])

    def project_video(n, carry):
        @pl.when(n < 7)
        def _():
            arrive(2 * n + 2)
            arrive(2 * n + 3)

        forward(2 * n).wait_recv()
        forward(2 * n + 1).wait_recv()
        at0 = (chip + 16 - 2 * n) % 16
        at1 = (chip + 15 - 2 * n) % 16
        normed = jnp.concatenate([norm(at0), norm(at1)], axis=0)
        for which in range(3):
            value = jnp.dot(
                normed, wpad[:, which * HP : (which + 1) * HP], preferred_element_type=F32
            )
            if which == 0:
                value = value * QSCALE
            if which == 2:
                value = jnp.where(vlane == E, 1.0, value)
            value = value.astype(BF)
            for h in range(4):
                piece = value[:, h * LANE : (h + 1) * LANE]
                heads[which, h, at0] = piece[:128]
                heads[which, h, at1] = piece[128:]
        keep_heads(2 * n).start()
        keep_heads(2 * n + 1).start()
        return carry

    lax.fori_loop(0, 6, project_video, 0)

    for copy in second:
        copy.wait_recv()
    for n in range(4):
        first = acc[n, y, :, 0:HALF]
        other = acc[z, n, :, HALF:DT]
        for j in range(3):
            first = first + r2[0, j, n].astype(F32)
            other = other + r2[1, j, n].astype(F32)
        part[0, n] = first
        part[1, n] = other
        s3[0, n] = first.astype(BF)
        s3[1, n] = other.astype(BF)
    third = []
    for j in range(1, 4):
        ty = (y + j) % 4
        tz = (z + j) % 4
        third.append(
            remote(
                s3.at[0, tz],
                r3.at[0, j - 1],
                r_send.at[6 + j],
                r_recv.at[6 + j],
                8 * tz + 2 * y + core,
            )
        )
        third.append(
            remote(
                s3.at[1, ty],
                r3.at[1, j - 1],
                r_send.at[9 + j],
                r_recv.at[9 + j],
                8 * z + 2 * ty + core,
            )
        )
    for copy in third:
        copy.start()
    lax.fori_loop(6, 8, project_video, 0)
    keep = pltpu.make_async_copy(vid.at[pl.ds(8 * quarter, 8)], quarter_out, o_sem)
    keep.start()

    for copy in third:
        copy.wait_recv()
    first = part[0, z]
    other = part[1, y]
    for j in range(3):
        first = first + r3[0, j].astype(F32)
        other = other + r3[1, j].astype(F32)
    enc_out[:, 0:HALF] = (cap_in[:, 0:HALF].astype(F32) + first).astype(BF)
    enc_out[:, HALF:DT] = (cap_in[:, HALF:DT].astype(F32) + other).astype(BF)

    keep.wait()
    pair.wait_send()
    for copy in second + third:
        copy.wait_send()

    def drain(i, carry):
        send_video(i).wait_send()
        forward(i).wait_send()
        return carry

    lax.fori_loop(1, 16, drain, 0)
    forward(0).wait_send()

    def drain_heads(i, carry):
        keep_heads(i).wait()
        return carry

    lax.fori_loop(0, 16, drain_heads, 0)


def attend_kernel(
    lengths,
    clip_order,
    enc_in,
    mod,
    wkv,
    heads_in,
    residual_in,
    wo,
    wcq,
    wco,
    out,
    heads,
    enc,
    mix,
    outw,
    win,
    ctx4,
    sel,
    kv,
    select,
    query,
    done,
    cross,
    hidden,
    residual,
    wob,
    wcqb,
    wcob,
    w_sem,
    h_send,
    h_recv,
    x_send,
    x_recv,
    c_send,
    c_recv,
    p_send,
    p_recv,
    q_send,
    q_recv,
    o_send,
    o_recv,
):
    seq, core, chip, y, z = place()
    grp = lax.axis_index("grp")
    sib = seq + 1 - 2 * core
    quarter = seq % 4
    clip = seq // 4
    barrier = pltpu.get_barrier_semaphore()

    heads_load = pltpu.make_async_copy(heads_in, heads, w_sem.at[8])
    heads_load.start()

    def greet_one(i, carry):
        greet((seq + i) % 32)
        return carry

    lax.fori_loop(1, 32, greet_one, 0)
    for j in range(1, 4):
        greet((grp + j) % 4, "grp")
    enc[z, y, core] = enc_in[...]
    kv[:, :, EP:LANE, :] = jnp.zeros((16, 2, LANE - EP, KEYS), BF)
    captions = [jnp.int32(0)] * 8
    for i in range(32):
        which = clip_order[i] - grp * 8
        captions = [jnp.where(which == c, i, found) for c, found in enumerate(captions)]
    pl.semaphore_wait(barrier, 34)
    again = Gather(enc, h_send, h_recv)
    again.start()
    loads = [
        pltpu.make_async_copy(wo.at[:, pl.ds(n * WIN, WIN)], wob.at[n], w_sem.at[n])
        for n in range(3)
    ]
    for n in range(3):
        loads.append(
            pltpu.make_async_copy(wcq.at[:, pl.ds(n * WIN, WIN)], wcqb.at[n], w_sem.at[3 + n])
        )
    loads.append(pltpu.make_async_copy(wco, wcob, w_sem.at[6]))
    loads.append(pltpu.make_async_copy(residual_in, residual, w_sem.at[7]))
    for copy in loads:
        copy.start()
    for n in range(4):
        select[n] = head_select(32 * n)
    gate = mod[2, pl.ds(clip, 1), :]

    def cross_x(j):
        mine = ctx4.at[grp]
        return remote(mine, mine, x_send.at[j - 1], x_recv.at[j - 1], (grp + j) % 4, "grp")

    def send_ctx(i):
        to = (chip + i) % 16
        return remote(
            sel.at[to // 2],
            kv.at[chip, core, pl.ds(0, EP)],
            c_send.at[i],
            c_recv.at[i],
            2 * to + core,
        )

    own_ctx = pltpu.make_async_copy(sel.at[clip], kv.at[chip, core, pl.ds(0, EP)], c_send.at[0])

    def share(i):
        rows = kv.at[(chip + 16 - i) % 16, core, pl.ds(0, EP)]
        return remote(rows, rows, p_send.at[i], p_recv.at[i], sib)

    def make_context():
        again.finish()

        def one(n, total):
            at = pl.multiple_of(n * 512, 512)
            left = enc[:, :, :, :, pl.ds(at, 512)].reshape(KEYS, 512)
            return total + lax.dot_general(
                wkv[:, pl.ds(at, 512)],
                left,
                (((1,), (1,)), ((), ())),
                preferred_element_type=F32,
            )

        turned = lax.fori_loop(0, 8, one, jnp.zeros((E, KEYS), F32))
        tail = lax.broadcasted_iota(jnp.int32, (EP - E, KEYS), 0)
        tail = jnp.where(tail == 0, 1.0, 0.0)
        ctx4[grp] = jnp.concatenate([turned, tail], axis=0).astype(BF)
        for j in range(1, 4):
            cross_x(j).start()

    def spread_context():
        for j in range(1, 4):
            cross_x(j).wait_recv()

        for c in range(8):
            sel[c] = ctx4[captions[c] // 8]
        own_ctx.start()

        def one(i, carry):
            send_ctx(i).start()
            return carry

        lax.fori_loop(1, 16, one, 0)

    def share_context():
        own_ctx.wait()
        share(0).start()

        def one(i, carry):
            send_ctx(i).wait_recv()
            share(i).start()
            return carry

        lax.fori_loop(1, 16, one, 0)

        def got(i, carry):
            share(i).wait()
            return carry

        lax.fori_loop(0, 16, got, 0)

    def at_step(step, when, work):
        @pl.when(step == when)
        def _():
            work()

    locals_of = {
        "middle": again.middle,
        "last": again.last,
        "context": make_context,
        "spread": spread_context,
    }

    def send_win(j):
        to = 4 * clip + (quarter + j) % 4
        return remote(outw.at[j], win.at[quarter], q_send.at[j], q_recv.at[j], to)

    own_win = pltpu.make_async_copy(outw.at[0], win.at[quarter], q_send.at[0])

    def attend(step, carry):
        j = (step // 2 + 1) % 4
        at = 4 * ((quarter + j) % 4)
        for u in range(2):
            h = 2 * (step % 2) + u
            q_rows = heads[0, h, pl.ds(at, 4)].reshape(512, LANE)
            key_rows = heads[1, h].reshape(VT, LANE)
            value_rows = heads[2, h].reshape(VT, LANE)
            score = lax.dot_general(
                q_rows, key_rows, (((1,), (1,)), ((), ())), preferred_element_type=F32
            )
            weight = jnp.exp2(score - jnp.max(score, axis=-1, keepdims=True)).astype(BF)
            value = jnp.dot(weight, value_rows, preferred_element_type=F32)
            value = value / value[:, E : E + 1]
            mix[h] = value.astype(BF)

        @pl.when(step % 2 == 1)
        def _():
            flat = jnp.concatenate([mix[h] for h in range(4)], axis=1)
            outw[j] = lax.dot_general(
                flat, select[quarter], (((1,), (1,)), ((), ())), preferred_element_type=F32
            ).astype(BF)

        @pl.when((step % 2 == 1) & (j > 0))
        def _():
            send_win(j).start()

        for when, work in ATTEND_STEPS:
            at_step(step, when, locals_of[work])
        return carry

    heads_load.wait()
    lax.fori_loop(0, 8, attend, 0)
    own_win.start()

    caption = captions[0]
    for c in range(1, 8):
        caption = jnp.where(clip == c, captions[c], caption)
    pack = caption // 8
    item = caption % 8
    begin = jnp.int32(0)
    finish = jnp.int32(0)
    for n in range(8):
        size = lengths[pack, n]
        begin = begin + jnp.where(n < item, size, 0)
        finish = finish + jnp.where(n <= item, size, 0)
    for copy in loads:
        copy.wait()
    own_win.wait()
    for j in range(1, 4):
        send_win(j).wait()

    def before(n, carry):
        at = pl.multiple_of(256 * n, 256)
        for c in range(3):
            cols = slice(c * WIN, (c + 1) * WIN)
            update = jnp.dot(
                win[0, pl.ds(at, 256)], wob[c, 0:WIN], preferred_element_type=F32
            )
            for i in range(1, 4):
                update = update + jnp.dot(
                    win[i, pl.ds(at, 256)],
                    wob[c, 256 * i : 256 * i + WIN],
                    preferred_element_type=F32,
                )
            first_rows = residual[pl.ds(4 * n, 4), :, cols].reshape(256, WIN)
            hidden[pl.ds(at, 256), cols] = (
                first_rows.astype(F32) + gate[:, cols] * update
            ).astype(BF)
        for c in range(3):
            value = jnp.dot(
                hidden[pl.ds(at, 256)], wcqb[c], preferred_element_type=F32
            )
            query[pl.ds(4 * n, 4), :, c * WIN : (c + 1) * WIN] = (
                (value * QSCALE).astype(BF).reshape(4, 64, WIN)
            )
        for i in range(4):
            cross[i, pl.ds(at, 256)] = jnp.dot(
                query[pl.ds(4 * n, 4), :, 256 * i : 256 * i + WIN].reshape(256, WIN),
                select[i],
                preferred_element_type=F32,
            ).astype(BF)
        return carry

    lax.fori_loop(0, 2, before, 0)
    share_context()

    def send(b):
        return remote(done.at[b], out.at[clip], o_send.at[b], o_recv.at[clip], 8 * quarter + b)

    def send_own(b):
        return pltpu.make_async_copy(done.at[b], out.at[clip], o_send.at[b])

    key_at = lax.broadcasted_iota(jnp.int32, (256, KEYS), 1)
    keep = (key_at >= begin) & (key_at < finish)

    def after(n, carry):
        at = pl.multiple_of(256 * n, 256)

        def four(i, carry):
            for h in range(4):
                at_head = 2 * i + h // 2
                lanes = slice(h * LANE, (h + 1) * LANE)
                score = jnp.dot(
                    cross[i, pl.ds(at, 256), lanes],
                    kv[at_head, h % 2],
                    preferred_element_type=F32,
                )
                score = jnp.where(keep, score, -1e30)
                weight = jnp.exp2(score - jnp.max(score, axis=-1, keepdims=True)).astype(BF)
                value = lax.dot_general(
                    weight,
                    kv[8 + at_head, h % 2],
                    (((1,), (1,)), ((), ())),
                    preferred_element_type=F32,
                )
                value = value / value[:, E : E + 1]
                cross[i, pl.ds(at, 256), lanes] = value.astype(BF)
            return carry

        lax.fori_loop(0, 4, four, 0)
        total = hidden[pl.ds(at, 256)].astype(F32)
        for i in range(4):
            window = lax.dot_general(
                cross[i, pl.ds(at, 256)],
                select[i],
                (((1,), (1,)), ((), ())),
                preferred_element_type=F32,
            ).astype(BF)
            total = total + jnp.dot(
                window, wcob[256 * i : 256 * i + WIN], preferred_element_type=F32
            )
        done[pl.ds(4 * n, 4)] = total.astype(BF).reshape(4, 64, D)
        for i in range(4):
            b = 4 * n + i

            @pl.when(8 * quarter + b == seq)
            def _():
                send_own(b).start()

            @pl.when(8 * quarter + b != seq)
            def _():
                send(b).start()

        return carry

    lax.fori_loop(0, 2, after, 0)

    for j in range(1, 4):
        cross_x(j).wait_send()

    def drain(i, carry):
        send_ctx(i).wait_send()
        return carry

    lax.fori_loop(1, 16, drain, 0)

    def drain_out(b, carry):
        @pl.when(8 * quarter + b == seq)
        def _():
            send_own(b).wait()

        @pl.when(8 * quarter + b != seq)
        def _():
            send(b).wait_send()

        @pl.when(4 * b + z != seq)
        def _():
            remote(done.at[0], out.at[b], o_send.at[0], o_recv.at[b], 4 * b + z).wait_recv()

        return carry

    lax.fori_loop(0, 8, drain_out, 0)


def params(number):
    return pltpu.CompilerParams(
        collective_id=number, has_side_effects=True, vmem_limit_bytes=58 * MIB
    )


def per_device(
    captions,
    lengths,
    clip_order,
    t5_gain,
    w_tq,
    w_tk,
    w_tv,
    w_to,
    w_kv,
    video,
    modulation,
    w_qkv,
    w_o,
    w_cq,
    w_co,
):
    vmem = pl.BlockSpec(memory_space=pltpu.VMEM)
    smem = pl.BlockSpec(memory_space=pltpu.SMEM)
    anywhere = pl.BlockSpec(memory_space=pl.ANY)
    dma = pltpu.SemaphoreType.DMA
    mods = jnp.transpose(modulation, (1, 0, 2))
    heads, quarter_rows, encoded = pl.pallas_call(
        front_kernel,
        out_shape=(
            jax.ShapeDtypeStruct((3, 4, 16, 128, LANE), BF),
            jax.ShapeDtypeStruct((8, 64, D), BF),
            jax.ShapeDtypeStruct((16, DT), BF),
        ),
        in_specs=[smem, vmem, vmem, vmem] + [anywhere] * 6,
        out_specs=(anywhere, anywhere, vmem),
        scratch_shapes=[
            pltpu.VMEM((3, 4, 16, 128, LANE), BF),
            pltpu.VMEM((4, 4, 2, 16, DT), BF),
            pltpu.VMEM((DT, 384), BF),
            pltpu.VMEM((128, DT), BF),
            pltpu.VMEM((3, D, WIN), BF),
            pltpu.VMEM((D, 3 * HP), BF),
            pltpu.VMEM((32, 64, D), BF),
            pltpu.VMEM((KEYS, 384), F32),
            pltpu.VMEM((4, 4, 2, 16, LANE), BF),
            pltpu.VMEM((4, 4, 16, DT), BF),
            pltpu.VMEM((4, 4, 16, DT), BF),
            pltpu.VMEM((4, 4, 16, DT), F32),
            pltpu.VMEM((4, 4, 16, DT), BF),
            pltpu.VMEM((2, 3, 4, 16, HALF), BF),
            pltpu.VMEM((2, 4, 16, HALF), F32),
            pltpu.VMEM((2, 4, 16, HALF), BF),
            pltpu.VMEM((2, 3, 16, HALF), BF),
            dma((8,)),
            dma((20,)),
            dma((20,)),
            dma((16,)),
            dma((16,)),
            dma((16,)),
            dma((16,)),
            dma((13,)),
            dma((13,)),
            dma,
            dma((16,)),
        ],
        compiler_params=params(0),
        name="front",
    )(
        lengths,
        t5_gain.reshape(1, DT),
        captions,
        mods,
        video,
        w_tq,
        w_tk,
        w_tv,
        w_to,
        w_qkv,
    )
    counts = (9, 20, 20, 3, 3, 16, 16, 16, 16, 4, 4, 8, 8)
    return pl.pallas_call(
        attend_kernel,
        out_shape=jax.ShapeDtypeStruct((8, 64, D), BF),
        in_specs=[smem, smem, vmem, vmem, vmem] + [anywhere] * 5,
        out_specs=anywhere,
        scratch_shapes=[
            pltpu.VMEM((3, 4, 16, 128, LANE), BF),
            pltpu.VMEM((4, 4, 2, 16, DT), BF),
            pltpu.VMEM((4, 512, LANE), BF),
            pltpu.VMEM((4, 512, WIN), BF),
            pltpu.VMEM((4, 512, WIN), BF),
            pltpu.VMEM((4, EP, KEYS), BF),
            pltpu.VMEM((8, EP, KEYS), BF),
            pltpu.VMEM((16, 2, LANE, KEYS), BF),
            pltpu.VMEM((4, WIN, HP), BF),
            pltpu.VMEM((8, 64, D), BF),
            pltpu.VMEM((8, 64, D), BF),
            pltpu.VMEM((4, 512, HP), BF),
            pltpu.VMEM((512, D), BF),
            pltpu.VMEM((8, 64, D), BF),
            pltpu.VMEM((3, D, WIN), BF),
            pltpu.VMEM((3, D, WIN), BF),
            pltpu.VMEM((D, D), BF),
        ]
        + [dma((n,)) if n else dma for n in counts],
        compiler_params=params(1),
        name="attend",
    )(
        lengths,
        clip_order,
        encoded,
        mods,
        w_kv.T,
        heads,
        quarter_rows,
        w_o,
        w_cq,
        w_co,
    )


def solution(mesh):
    in_specs = (
        P(("grp", "seq"), None),
        P(),
        P(),
        P(),
        P(None, "seq"),
        P(None, "seq"),
        P(None, "seq"),
        P("seq", None),
        P(None, "seq"),
        P("grp", "seq", None),
        P("grp", None, None),
        P(),
        P(),
        P(),
        P(),
    )
    out_specs = P("grp", "seq", None)
    return jax.shard_map(
        per_device, mesh=mesh, in_specs=in_specs, out_specs=out_specs, check_vma=False
    )
```
